32 devices in a mesh: groups: 2 (over x), dp: 2 (over core), ctx: 8 (over z, y).
Axes of the slice: x: 2, y: 2, z: 4, core: 2. Of those that a mesh axis runs over, the one named last changes fastest.
Arguments:
- queries: bfloat16 [4, 1024, 4096], P(('groups', 'dp'), 'ctx'), parts along dimension 0, may hold values from -16 to 16
- key_matrix: bfloat16 [4, 1024, 512], P(('groups', 'dp'), 'ctx'), parts along dimension 0, may hold values from -16 to 16
- value_matrix: bfloat16 [4, 1024, 512], P(('groups', 'dp'), 'ctx'), parts along dimension 0, may hold values from -6 to 6
- cotangent: bfloat16 [4, 1024, 4096], P(('groups', 'dp'), 'ctx'), parts along dimension 0, may hold values from -6 to 6
- segment: int32 [4, 1024], P(('groups', 'dp'), 'ctx'), parts along dimension 0, may hold values from 0 to 3, never falling along the last dimension, each value on 1 to 512 neighbouring positions
Outputs:
- attended: bfloat16 [4, 1024, 4096], P(('groups', 'dp'), 'ctx'), parts along dimension 0
- grad_query: float32 [4, 1024, 4096], P(('groups', 'dp'), 'ctx'), parts along dimension 0
- key_gradient_rows: float32 [4, 1024, 512], P(('groups', 'dp'), 'ctx'), parts along dimension 0
- value_gradient_rows: float32 [4, 1024, 512], P(('groups', 'dp'), 'ctx'), parts along dimension 0
The draws below stay inside these ranges and needn't reach their ends.
There are 2 independent parts, one for each index of `groups`. The reference program is written for one: setup_inputs(seed, part) draws one part's arguments, and reference() takes and returns one part's arrays. A program takes and returns all parts, laid end to end along the dimension named above; each array names one. Nothing has to cross between parts.
All inputs are finite; a program needn't handle non-finite values.
Results may differ from the reference program's by a relative error of at most 0.04.
Values may be sent and summed in bfloat16 or wider, within the bound.
No kernel may reach another device: no remote copies, remote signals or barrier semaphores. Data moves between devices by JAX's collectives and lax.ppermute only.
A program may use at most 128 MiB of HBM per device.

```python
import math
import jax
import jax.numpy as jnp
import numpy as np
from jax import lax

QUERY_HEADS = 32
KEY_VALUE_HEADS = 4
HEAD_WIDTH = 128
STREAM_LENGTH = 1024
DOC_MOST = 512
DOCS = 4
N_DP = 2


def draw_queries(key, part):
    key = jax.random.fold_in(key, 5)
    coarse_estimate = jax.random.normal(key, (N_DP, STREAM_LENGTH, QUERY_HEADS, HEAD_WIDTH), jnp.float32)
    return jnp.clip(coarse_estimate, -16.0, 16.0).reshape(N_DP, STREAM_LENGTH, QUERY_HEADS * HEAD_WIDTH).astype(jnp.bfloat16)


def draw_key_matrix(key, part):
    key = jax.random.fold_in(key, 9)
    coarse_estimate = jax.random.normal(key, (N_DP, STREAM_LENGTH, KEY_VALUE_HEADS, HEAD_WIDTH), jnp.float32)
    return jnp.clip(coarse_estimate, -16.0, 16.0).reshape(N_DP, STREAM_LENGTH, KEY_VALUE_HEADS * HEAD_WIDTH).astype(jnp.bfloat16)


def steps_of(stream_key, dims, cuts, least, top_value):
    gain = 1.0
    for axis_at, parts in cuts:
        steps = jax.random.uniform(jax.random.fold_in(jax.random.fold_in(stream_key, 6), axis_at), (parts,), jnp.float32, least / len(cuts), top_value / len(cuts))
        gain = gain * jnp.repeat(jnp.exp(steps), dims[axis_at] // parts).reshape((-1,) + (1,) * (len(dims) - 1 - axis_at))
    return gain


def split_up(amount, total, most, lean):
    portions = [(1 << 20) // math.isqrt(grade ** lean) + 1 for grade in range(2, amount + 1)]
    spare, given = total - most - (amount - 1), [1] * (amount - 1)
    while spare > 0:
        movable = [i for i in range(amount - 1) if given[i] < most]
        mass, left = sum([portions[i] for i in movable]), spare
        for i in movable:
            addition = min(most - given[i], max(1, left * portions[i] // mass), spare)
            given[i] = given[i] + addition
            spare = spare - addition
    return np.array([most] + given)


def uneven(own_key, count, total, limit, skew):
    if count == 2:
        one = jax.random.randint(own_key, (), max(1, total - limit), min(limit, total - 1) + 1)
        return jnp.stack([one, total - one])
    sizes = jnp.asarray(split_up(count, total, limit, skew), jnp.int32)
    twos = (count - 1) // 2
    source_of, receiver = sizes[1:1 + 2 * twos:2], sizes[2:2 + 2 * twos:2]
    margin = jnp.minimum(source_of - 1, limit - receiver)
    passed = jax.random.randint(jax.random.fold_in(own_key, 1), (twos,), 0, 1 << 20) % (margin + 1)
    sizes = sizes.at[1:1 + 2 * twos:2].set(source_of - passed).at[2:2 + 2 * twos:2].set(receiver + passed)
    return sizes[jax.random.permutation(jax.random.fold_in(own_key, 2), count)]


def centred(stream_key, shape, width, limit, cuts=(), kind=jnp.bfloat16):
    values = jax.random.normal(stream_key, shape, jnp.float32) * width
    if len(cuts) > 0:
        values = steps_of(stream_key, shape, cuts, -0.22, 0.18) * values
    return jnp.clip(values, min=-limit, max=limit).astype(kind)


def setup_inputs(seed: int = 0, part: int = 0) -> dict:
    streams_of = jax.random.split(jax.random.key(seed), 6)
    part_keys = jax.random.split(jax.random.fold_in(streams_of[5], part), 6)
    return {
        "queries": draw_queries(jax.random.fold_in(jax.random.fold_in(streams_of[5], part), 71), part),
        "key_matrix": draw_key_matrix(jax.random.fold_in(jax.random.fold_in(streams_of[5], part), 71), part),
        "value_matrix": centred(part_keys[2], (N_DP, STREAM_LENGTH, KEY_VALUE_HEADS * HEAD_WIDTH), 1.0, 6.0, ((0, 2), (1, 8))),
        "cotangent": centred(part_keys[3], (N_DP, STREAM_LENGTH, QUERY_HEADS * HEAD_WIDTH), 1.0, 6.0, ((0, 2), (1, 8))),
        "segment": jax.vmap(lambda own: jnp.searchsorted(jnp.cumsum(uneven(own, DOCS, STREAM_LENGTH, DOC_MOST, 1)), jnp.arange(STREAM_LENGTH), side="right"))(jax.random.split(part_keys[4], N_DP)).reshape((N_DP, STREAM_LENGTH)).astype(jnp.int32),
    }


def one_stream(queries, key_matrix, value_matrix, cotangent, segment):
    block_size = queries.shape[0]
    query_group = QUERY_HEADS // KEY_VALUE_HEADS
    scale = 1.0 / math.sqrt(HEAD_WIDTH)
    highest = lax.Precision.HIGHEST
    every_query = queries.reshape(block_size, KEY_VALUE_HEADS, query_group, HEAD_WIDTH).transpose(1, 0, 2, 3)
    gradient_rows = cotangent.reshape(block_size, KEY_VALUE_HEADS, query_group, HEAD_WIDTH).transpose(1, 0, 2, 3)
    every_key = key_matrix.reshape(block_size, KEY_VALUE_HEADS, HEAD_WIDTH).transpose(1, 0, 2)
    every_value = value_matrix.reshape(block_size, KEY_VALUE_HEADS, HEAD_WIDTH).transpose(1, 0, 2)
    places = jnp.arange(block_size, dtype=jnp.int32)
    allowed = (places[None, :] <= places[:, None]) & ((segment[None, :] == segment[:, None]) | (segment[None, :] == 0))

    def per_head(items):
        q_head, k_head, v_head, d_head = items
        q_f = q_head.astype(jnp.float32)
        k_f = k_head.astype(jnp.float32)
        v_f = v_head.astype(jnp.float32)
        d_f = d_head.astype(jnp.float32)
        logits = jnp.einsum('tgd,sd->gts', q_f, k_f, precision=highest) * scale
        logits = jnp.where(allowed[None], logits, jnp.float32(-1e+30))
        top = lax.optimization_barrier(jnp.max(logits, axis=-1))
        expd = jnp.where(allowed[None], jnp.exp(logits - top[..., None]), jnp.float32(0.0))
        total = lax.optimization_barrier(jnp.sum(expd, axis=-1))
        log_sum = top + jnp.log(total)
        probs = jnp.where(allowed[None], jnp.exp(logits - log_sum[..., None]), jnp.float32(0.0))
        probs_b = lax.optimization_barrier(probs.astype(jnp.bfloat16)).astype(jnp.float32)
        outv = jnp.einsum('gts,sd->tgd', probs_b, v_f, precision=highest)
        out_b = outv.astype(jnp.bfloat16)
        delta = lax.optimization_barrier(jnp.sum(d_f * out_b.astype(jnp.float32), axis=-1)).T
        value_gradient = jnp.einsum('gts,tgd->sd', probs_b, d_f, precision=highest)
        along = jnp.einsum('tgd,sd->gts', d_f, v_f, precision=highest)
        slopes = lax.optimization_barrier((probs * (along - delta[..., None])).astype(jnp.bfloat16)).astype(jnp.float32)
        grad_q = scale * jnp.einsum('gts,sd->tgd', slopes, k_f, precision=highest)
        key_gradient = scale * jnp.einsum('gts,tgd->sd', slopes, q_f, precision=highest)
        return (out_b, grad_q, key_gradient, value_gradient)
    out_b, grad_q, key_gradient, value_gradient = lax.map(per_head, (every_query, every_key, every_value, gradient_rows))
    out_b = out_b.transpose(1, 0, 2, 3).reshape(block_size, QUERY_HEADS * HEAD_WIDTH)
    grad_q = grad_q.transpose(1, 0, 2, 3).reshape(block_size, QUERY_HEADS * HEAD_WIDTH)
    key_gradient = key_gradient.transpose(1, 0, 2).reshape(block_size, KEY_VALUE_HEADS * HEAD_WIDTH)
    value_gradient = value_gradient.transpose(1, 0, 2).reshape(block_size, KEY_VALUE_HEADS * HEAD_WIDTH)
    return (out_b, grad_q, key_gradient, value_gradient)

def reference(queries, key_matrix, value_matrix, cotangent, segment):
    results = [one_stream(queries[index], key_matrix[index], value_matrix[index], cotangent[index], segment[index]) for index in range(N_DP)]
    attended = jnp.stack([item[0] for item in results])
    grad_query = jnp.stack([item[1] for item in results])
    key_gradient_rows = jnp.stack([item[2] for item in results])
    value_gradient_rows = jnp.stack([item[3] for item in results])
    return (attended, grad_query, key_gradient_rows, value_gradient_rows)
```

```python
import functools
import math

import jax
import jax.numpy as jnp
from jax import lax
from jax.experimental import pallas as pl
from jax.experimental.pallas import tpu as pltpu
from jax.sharding import PartitionSpec as P

KV = 4
D = 128
CHUNKS = 1
NEG = -1e30
NN = (((1,), (0,)), ((), ()))
NT = (((1,), (1,)), ((), ()))
TN = (((0,), (0,)), ((), ()))


def dot(a, b, dims):
    return lax.dot_general(a, b, dims, preferred_element_type=jnp.float32)


def pack_kernel(k_ref, v_ref, s_ref, *outs):
    rows = k_ref.shape[1]
    per = KV // len(outs)
    seg = jnp.broadcast_to(s_ref[...].astype(jnp.float32), (16, rows)).astype(jnp.bfloat16)
    for c, out in enumerate(outs):
        for g in range(per):
            cols = slice((c * per + g) * D, (c * per + g + 1) * D)
            out[2 * g * rows : (2 * g + 1) * rows, :] = k_ref[0, :, cols]
            out[(2 * g + 1) * rows : (2 * g + 2) * rows, :] = v_ref[0, :, cols]
        out[2 * per * rows :, :] = seg


def attend_kernel(pairs, per, has_prev, here_ref, *refs):
    own = refs[:pairs]
    peer = refs[pairs : 2 * pairs]
    q_ref, c_ref, sq_ref = refs[2 * pairs : 2 * pairs + 3]
    refs = refs[2 * pairs + 3 + (2 if has_prev else 0) :]
    out_ref, gq_ref, mine_ref, theirs_ref = refs[:4]
    kv, mask, e_scr, cnt, order = refs[4:]
    rows = q_ref.shape[1]
    heads = q_ref.shape[2] // D
    wide = heads * rows
    scale = 1.0 / math.sqrt(D)
    power = scale * math.log2(math.e)
    g = pl.program_id(0)
    here = here_ref[0]

    @pl.when(g == 0)
    def _():
        seg_q = sq_ref[...].astype(jnp.float32)
        q_pos = here * rows + lax.broadcasted_iota(jnp.int32, (rows, rows), 1)
        local = lax.broadcasted_iota(jnp.int32, (rows, rows), 0)
        cnt[0] = 0
        for k in range(pairs):
            live = jnp.float32(0.0)
            for lane, src in enumerate((own[k], peer[k])):
                block = (here ^ lane) - 2 * k
                seg_row = src[2 * per * rows : 2 * per * rows + 16, :].astype(jnp.float32)
                seg_k = jnp.transpose(jnp.broadcast_to(seg_row[:1], (rows, rows)))
                ok = (block * rows + local <= q_pos) & ((seg_k == seg_q) | (seg_k == 0.0)) & (block >= 0)
                add = jnp.where(ok, 0.0, NEG)
                mask[k, lane * rows : (lane + 1) * rows, :] = add
                live = jnp.maximum(live, jnp.max(jnp.where(ok, 1.0, 0.0)))
                for h in range(per):
                    for part in range(2):
                        kv[k, h, part, lane * rows : (lane + 1) * rows, :] = src[
                            (2 * h + part) * rows : (2 * h + part + 1) * rows, :
                        ]

            @pl.when(live > 0.0)
            def _():
                order[cnt[0]] = k
                cnt[0] = cnt[0] + 1

    zero = jnp.zeros((2 * rows, D), jnp.float32)
    at = pl.multiple_of(g * 2 * rows, 2 * rows)
    for k in range(pairs):
        mine_ref[k, pl.ds(at, 2 * rows), :] = zero
        theirs_ref[k, pl.ds(at, 2 * rows), :] = zero.astype(jnp.bfloat16)

    def stack(ref):
        return jnp.concatenate([ref[0, :, h * D : (h + 1) * D] for h in range(heads)], axis=0)

    q_all = stack(q_ref)
    c_all = stack(c_ref)
    live_pairs = cnt[0]

    def scores(t, top):
        k = order[t]
        s = dot(kv[k, g, 0], q_all, NT)
        s = s + jnp.concatenate([mask[k]] * heads, axis=1)
        e_scr[k] = s
        return jnp.maximum(top, jnp.max(s, axis=0, keepdims=True))

    top = lax.fori_loop(0, live_pairs, scores, jnp.full((1, wide), NEG, jnp.float32))

    def forward(t, carry):
        total, acc = carry
        k = order[t]
        e = jnp.exp2((e_scr[k] - top) * power)
        e_scr[k] = e
        total = total + jnp.sum(e, axis=0, keepdims=True)
        return total, acc + dot(kv[k, g, 1], e.astype(jnp.bfloat16), TN)

    total, acc = lax.fori_loop(
        0, live_pairs, forward, (jnp.zeros((1, wide), jnp.float32), jnp.zeros((D, wide), jnp.float32))
    )
    inverse = 1.0 / total
    acc = acc * inverse
    deltas = []
    for h in range(heads):
        o = acc[:, h * rows : (h + 1) * rows]
        out_ref[0, :, h * D : (h + 1) * D] = jnp.transpose(o).astype(jnp.bfloat16)
        c_t = jnp.transpose(c_ref[0, :, h * D : (h + 1) * D].astype(jnp.float32))
        deltas.append(jnp.sum(c_t * o.astype(jnp.bfloat16).astype(jnp.float32), axis=0, keepdims=True))
    delta = jnp.concatenate(deltas, axis=1)

    def backward(t, acc):
        k = order[t]
        probs = e_scr[k] * inverse
        along = dot(kv[k, g, 1], c_all, NT)
        slopes = (probs * (along - delta)).astype(jnp.bfloat16)
        grad_v = dot(probs.astype(jnp.bfloat16), c_all, NN)
        grad_k = dot(slopes, q_all, NN) * scale
        mine_ref[k, pl.ds(at, rows), :] = grad_k[:rows]
        mine_ref[k, pl.ds(at + rows, rows), :] = grad_v[:rows]
        theirs_ref[k, pl.ds(at, rows), :] = grad_k[rows:].astype(jnp.bfloat16)
        theirs_ref[k, pl.ds(at + rows, rows), :] = grad_v[rows:].astype(jnp.bfloat16)
        return acc + dot(kv[k, g, 0], slopes, TN)

    grad = lax.fori_loop(0, live_pairs, backward, jnp.zeros((D, wide), jnp.float32)) * scale
    for h in range(heads):
        gq_ref[0, :, h * D : (h + 1) * D] = jnp.transpose(grad[:, h * rows : (h + 1) * rows])


def attend(chunk, here, own, peer, queries, cotangent, segment, prev):
    pairs = len(own)
    per = KV // CHUNKS
    _, rows, width = queries.shape
    block = width // KV
    wide = block // D * rows
    tall = own[0].shape
    whole = pl.BlockSpec(tall, lambda g: (0, 0))
    columns = pl.BlockSpec((1, rows, block), lambda g: (0, 0, chunk * per + g))
    parts = pl.BlockSpec((pairs, per * 2 * rows, D), lambda g: (0, 0, 0))
    args = [here, *own, *peer, queries, cotangent, segment]
    in_specs = [pl.BlockSpec(memory_space=pltpu.SMEM)] + [whole] * (2 * pairs)
    in_specs += [columns, columns, pl.BlockSpec(segment.shape, lambda g: (0, 0))]
    aliases = {}
    if prev is not None:
        aliases = {len(args): 0, len(args) + 1: 1}
        args += list(prev)
        in_specs += [pl.BlockSpec(memory_space=pl.ANY)] * 2
    macs = per * wide * 2 * rows * D * 6 * pairs
    return pl.pallas_call(
        functools.partial(attend_kernel, pairs, per, prev is not None),
        grid=(per,),
        in_specs=in_specs,
        out_specs=[columns, columns, parts, parts],
        out_shape=[
            jax.ShapeDtypeStruct(queries.shape, jnp.bfloat16),
            jax.ShapeDtypeStruct(queries.shape, jnp.float32),
            jax.ShapeDtypeStruct((pairs, per * 2 * rows, D), jnp.float32),
            jax.ShapeDtypeStruct((pairs, per * 2 * rows, D), jnp.bfloat16),
        ],
        scratch_shapes=[
            pltpu.VMEM((pairs, per, 2, 2 * rows, D), jnp.bfloat16),
            pltpu.VMEM((pairs, 2 * rows, rows), jnp.float32),
            pltpu.VMEM((pairs, 2 * rows, wide), jnp.float32),
            pltpu.SMEM((1,), jnp.int32),
            pltpu.SMEM((pairs,), jnp.int32),
        ],
        input_output_aliases=aliases,
        compiler_params=pltpu.CompilerParams(vmem_limit_bytes=56 << 20),
        cost_estimate=pl.CostEstimate(flops=4 * macs, bytes_accessed=8 << 20, transcendentals=0),
    )(*args)


def add_kernel(mine_ref, got_ref, keep_ref, *sends):
    keep_ref[...] = mine_ref[0] + got_ref[0].astype(jnp.float32)
    for k, send in enumerate(sends):
        send[...] = (mine_ref[k + 1] + got_ref[k + 1].astype(jnp.float32)).astype(jnp.bfloat16)


def add_lanes(mine, got):
    pairs, tall, _ = mine.shape
    return pl.pallas_call(
        add_kernel,
        out_shape=[jax.ShapeDtypeStruct((tall, D), jnp.float32)]
        + [jax.ShapeDtypeStruct((tall, D), jnp.bfloat16)] * (pairs - 1),
        cost_estimate=pl.CostEstimate(flops=mine.size, bytes_accessed=8 * mine.size, transcendentals=0),
        compiler_params=pltpu.CompilerParams(vmem_limit_bytes=48 << 20),
    )(mine, got)


def finish_kernel(pairs, *refs):
    ins, (gk_ref, gv_ref) = refs[:-2], refs[-2:]
    rows = gk_ref.shape[1]
    per = ins[0].shape[0] // (2 * rows)
    for c in range(len(ins) // pairs):
        chunk = ins[c * pairs : (c + 1) * pairs]
        for g in range(per):
            cols = slice((c * per + g) * D, (c * per + g + 1) * D)
            for part, out in enumerate((gk_ref, gv_ref)):
                span = slice((2 * g + part) * rows, (2 * g + part + 1) * rows)
                total = chunk[0][span, :]
                for ref in chunk[1:]:
                    total = total + ref[span, :].astype(jnp.float32)
                out[0, :, cols] = total


def per_device(size, queries, key_matrix, value_matrix, cotangent, segment):
    rows = queries.shape[1]
    pairs = size // 2
    per = KV // CHUNKS
    here = lax.axis_index("ctx").astype(jnp.int32).reshape(1)
    swap = [(i, i ^ 1) for i in range(size)]

    def send(x, perm):
        return lax.ppermute(x, "ctx", perm)

    packed = pl.pallas_call(
        pack_kernel,
        out_shape=[jax.ShapeDtypeStruct((per * 2 * rows + 16, D), jnp.bfloat16)] * CHUNKS,
    )(key_matrix, value_matrix, segment)

    prev = None
    finals = []
    for c in range(CHUNKS):
        own = [packed[c]] + [
            send(packed[c], [(i, i + 2 * k) for i in range(size - 2 * k)]) for k in range(1, pairs)
        ]
        peer = [send(x, swap) for x in own]
        attended, grad_query, mine, theirs = attend(
            c, here, own, peer, queries, cotangent, segment, prev
        )
        prev = (attended, grad_query)
        keep, *down = add_lanes(mine, send(theirs, swap))
        finals.append(keep)
        finals += [
            send(x, [(i + 2 * k, i) for i in range(size - 2 * k)]) for k, x in enumerate(down, 1)
        ]
    grads = pl.pallas_call(
        functools.partial(finish_kernel, pairs),
        out_shape=[jax.ShapeDtypeStruct(key_matrix.shape, jnp.float32)] * 2,
    )(*finals)
    return (attended, grad_query, grads[0], grads[1])


def solution(mesh):
    wide = P(("groups", "dp"), "ctx", None)
    return jax.shard_map(
        functools.partial(per_device, mesh.shape["ctx"]),
        mesh=mesh,
        in_specs=(wide, wide, wide, wide, P(("groups", "dp"), "ctx")),
        out_specs=(wide, wide, wide, wide),
        check_vma=False,
    )
```

```python
import functools
import math

import jax
import jax.numpy as jnp
from jax import lax
from jax.experimental import pallas as pl
from jax.experimental.pallas import tpu as pltpu
from jax.sharding import PartitionSpec as P

KV = 4
D = 128
CHUNKS = 2
BUNDLE = 4
LANES = 256
STEPS = 4
NEG = -1e30
NN = (((1,), (0,)), ((), ()))
NT = (((1,), (1,)), ((), ()))
TN = (((0,), (0,)), ((), ()))


def dot(a, b, dims):
    return lax.dot_general(a, b, dims, preferred_element_type=jnp.float32)


def pack_kernel(k_ref, v_ref, s_ref, *outs):
    rows = k_ref.shape[1]
    per = KV // len(outs)
    seg = jnp.broadcast_to(s_ref[...].astype(jnp.float32), (16, rows)).astype(jnp.bfloat16)
    for c, out in enumerate(outs):
        for g in range(per):
            cols = slice((c * per + g) * D, (c * per + g + 1) * D)
            out[2 * g * rows : (2 * g + 1) * rows, :] = k_ref[0, :, cols]
            out[(2 * g + 1) * rows : (2 * g + 2) * rows, :] = v_ref[0, :, cols]
        out[2 * per * rows :, :] = seg


def loop(count, body, start, pairs):
    if pairs <= BUNDLE:
        return body(0, start)
    return lax.fori_loop(0, count, body, start)


def attend_kernel(pairs, per, chunk, lanes, has_prev, here_ref, *refs):
    own = refs[:pairs]
    peer = refs[pairs : 2 * pairs]
    q_ref, c_ref, sq_ref = refs[2 * pairs : 2 * pairs + 3]
    refs = refs[2 * pairs + 3 + (2 if has_prev else 0) :]
    out_ref, gq_ref = refs[:2]
    parts = refs[2:8]
    kv, mask, s_scr, p_scr, e_scr, probs_scr, slopes_scr, out_scr, gq_scr, cnt, order, sems = refs[8:]
    rows = q_ref.shape[1]
    heads = q_ref.shape[2] // KV // D
    each = heads * D
    static = pairs <= BUNDLE
    wide = heads * rows
    two = 2 * rows
    tall = BUNDLE * two
    scale = 1.0 / math.sqrt(D)
    power = scale * math.log2(math.e)
    here = here_ref[0]

    seg_q = sq_ref[...].astype(jnp.float32)
    q_pos = here * rows + lax.broadcasted_iota(jnp.int32, (rows, rows), 1)
    local = lax.broadcasted_iota(jnp.int32, (rows, rows), 0)
    sources = [src for k in range(pairs) for src in (own[k], peer[k])]
    base = 2 * per * rows
    seg_rows = [src[base : base + 16, :].astype(jnp.float32)[:1] for src in sources]
    seg_rows.append(jnp.zeros((rows - len(sources), rows), jnp.float32))
    seg_cols = jnp.transpose(jnp.concatenate(seg_rows, axis=0))

    def masks(k):
        adds = []
        for lane in range(2):
            block = (here ^ lane) - 2 * k
            seg_k = seg_cols[:, 2 * k + lane : 2 * k + lane + 1]
            ok = (block * rows + local <= q_pos) & ((seg_k == seg_q) | (seg_k == 0.0)) & (block >= 0)
            adds.append(jnp.where(ok, 0.0, NEG))
        return adds

    def store(at, k, adds):
        for lane, src in enumerate((own[k], peer[k])):
            to = pl.ds(pl.multiple_of(at + lane * rows, rows), rows)
            mask[to, :] = adds[lane]
            for h in range(per):
                for part in range(2):
                    kv[h, part, to, :] = src[(2 * h + part) * rows : (2 * h + part + 1) * rows, :]

    if static:
        for k in range(pairs):
            store(k * two, k, masks(k))
    else:
        cnt[0] = 0
        for k in range(pairs):
            adds = masks(k)

            @pl.when(jnp.max(jnp.maximum(adds[0], adds[1])) == 0.0)
            def _():
                store(cnt[0] * two, k, adds)
                order[cnt[0]] = k
                cnt[0] = cnt[0] + 1

        def blank(t, carry):
            at = pl.ds(pl.multiple_of(t * two, two), two)
            mask[at, :] = jnp.full((two, rows), NEG, jnp.float32)
            kv[:, :, at, :] = jnp.zeros((per, 2, two, D), jnp.bfloat16)
            order[t] = -1
            return carry

        lax.fori_loop(cnt[0], pl.cdiv(cnt[0], BUNDLE) * BUNDLE, blank, 0)
        for ref in parts:
            ref[...] = jnp.zeros_like(ref)
    bundles = None if static else pl.cdiv(cnt[0], BUNDLE)
    copies = []

    def send(src, ref, g, which):
        to = ref.at[0, :, pl.ds((chunk * per + g) * each, each)]
        copy = pltpu.make_async_copy(src.at[g], to, sems.at[2 * g + which])
        copy.start()
        copies.append(copy)

    def stack(ref, g):
        first = (chunk * per + g) * heads
        return jnp.concatenate([ref[0, :, (first + h) * D : (first + h + 1) * D] for h in range(heads)], axis=0)

    def tile(t, j):
        step = tall // STEPS
        return pl.ds(pl.multiple_of(t * tall + j * step, step), step)

    def span_of(t):
        return pl.ds(pl.multiple_of(t * tall, tall), tall)

    def one_head(g):
        q_all = stack(q_ref, g)
        c_all = stack(c_ref, g)
        at = g * two
        for w in range(wide // lanes):
            cols = slice(w * lanes, (w + 1) * lanes)
            q_w, c_w = q_all[cols], c_all[cols]

            def scores(t, top, q_w=q_w, c_w=c_w):
                span = span_of(t)
                s = dot(kv[g, 0, span, :], q_w, NT)
                s = s + jnp.concatenate([mask[span, :]] * (lanes // rows), axis=1)
                s_scr[span, :] = s
                p_scr[span, :] = dot(kv[g, 1, span, :], c_w, NT)
                top = jnp.maximum(top, jnp.max(s, axis=0, keepdims=True))
                return top

            top = loop(bundles, scores, jnp.full((1, lanes), NEG, jnp.float32), pairs)

            def forward(t, carry, top=top):
                total, delta, acc = carry
                for j in range(STEPS):
                    at = tile(t, j)
                    e = jnp.exp2((s_scr[at, :] - top) * power)
                    s_scr[at, :] = e
                    e_scr[at, :] = e.astype(jnp.bfloat16)
                    total = total + jnp.sum(e, axis=0, keepdims=True)
                    delta = delta + jnp.sum(e * p_scr[at, :], axis=0, keepdims=True)
                span = span_of(t)
                return total, delta, acc + dot(kv[g, 1, span, :], e_scr[span, :], TN)

            row = jnp.zeros((1, lanes), jnp.float32)
            total, delta, acc = loop(bundles, forward, (row, row, jnp.zeros((D, lanes), jnp.float32)), pairs)
            inverse = 1.0 / total
            delta = delta * inverse
            acc = acc * inverse
            for h in range(lanes // rows):
                to = slice((w * lanes // rows + h) * D, (w * lanes // rows + h + 1) * D)
                out_scr[g, :, to] = jnp.transpose(acc[:, h * rows : (h + 1) * rows]).astype(jnp.bfloat16)

            def backward(t, acc, inverse=inverse, delta=delta, cols=cols):
                for j in range(STEPS):
                    at = tile(t, j)
                    probs = s_scr[at, :] * inverse
                    probs_scr[at, cols] = probs.astype(jnp.bfloat16)
                    slopes_scr[at, cols] = (probs * (p_scr[at, :] - delta)).astype(jnp.bfloat16)
                span = span_of(t)
                return acc + dot(kv[g, 0, span, :], slopes_scr[span, cols], TN)

            grad = loop(bundles, backward, jnp.zeros((D, lanes), jnp.float32), pairs) * scale
            for h in range(lanes // rows):
                to = slice((w * lanes // rows + h) * D, (w * lanes // rows + h + 1) * D)
                gq_scr[g, :, to] = jnp.transpose(grad[:, h * rows : (h + 1) * rows])

        send(out_scr, out_ref, g, 0)
        send(gq_scr, gq_ref, g, 1)

        def key_side(t, carry):
            span = span_of(t)
            all_v = dot(probs_scr[span, :], c_all, NN)
            all_k = dot(slopes_scr[span, :], q_all, NN) * scale
            for j in range(BUNDLE):
                k = None if static else order[t * BUNDLE + j]
                grad_v = all_v[j * two : (j + 1) * two]
                grad_k = all_k[j * two : (j + 1) * two]

                def keep(first, slot):
                    for lane, ref in enumerate(parts[first : first + 2]):
                        part = slice(lane * rows, (lane + 1) * rows)
                        ref[slot, pl.ds(at, rows), :] = grad_k[part].astype(ref.dtype)
                        ref[slot, pl.ds(at + rows, rows), :] = grad_v[part].astype(ref.dtype)

                if static:
                    keep(*((0, 0) if j == 0 else (4, 0) if j == pairs - 1 else (2, j - 1)))
                    continue
                pl.when(k == 0)(lambda: keep(0, 0))
                pl.when((k > 0) & (k < pairs - 1))(lambda: keep(2, k - 1))
                pl.when(k == pairs - 1)(lambda: keep(4, 0))
            return carry

        loop(bundles, key_side, 0, pairs)

    for g in range(per):
        one_head(g)
    for copy in copies:
        copy.wait()


def attend(chunk, here, own, peer, queries, cotangent, segment, prev):
    pairs = len(own)
    per = KV // CHUNKS
    _, rows, width = queries.shape
    each = width // KV
    wide = each // D * rows
    lanes = wide if pairs <= BUNDLE else LANES
    keys = pl.cdiv(pairs, BUNDLE) * BUNDLE * 2 * rows
    vmem = pl.BlockSpec(memory_space=pltpu.VMEM)
    hbm = pl.BlockSpec(memory_space=pl.ANY)
    parts = [
        jax.ShapeDtypeStruct((count, per * 2 * rows, D), dtype)
        for count, dtype in (
            (1, jnp.float32),
            (1, jnp.float32),
            (pairs - 2, jnp.float32),
            (pairs - 2, jnp.bfloat16),
            (1, jnp.bfloat16),
            (1, jnp.bfloat16),
        )
    ]
    args = [here, *own, *peer, queries, cotangent, segment]
    in_specs = [pl.BlockSpec(memory_space=pltpu.SMEM)] + [vmem] * (len(args) - 1)
    aliases = {}
    if prev is not None:
        aliases = {len(args): 0, len(args) + 1: 1}
        args += list(prev)
        in_specs += [hbm] * 2
    macs = per * wide * 2 * rows * D * 6 * pairs
    return pl.pallas_call(
        functools.partial(attend_kernel, pairs, per, chunk, lanes, prev is not None),
        in_specs=in_specs,
        out_specs=[hbm, hbm] + [vmem] * len(parts),
        out_shape=[
            jax.ShapeDtypeStruct(queries.shape, jnp.bfloat16),
            jax.ShapeDtypeStruct(queries.shape, jnp.float32),
            *parts,
        ],
        scratch_shapes=[
            pltpu.VMEM((per, 2, keys, D), jnp.bfloat16),
            pltpu.VMEM((keys, rows), jnp.float32),
            pltpu.VMEM((keys, lanes), jnp.float32),
            pltpu.VMEM((keys, lanes), jnp.float32),
            pltpu.VMEM((keys, lanes), jnp.bfloat16),
            pltpu.VMEM((keys, wide), jnp.bfloat16),
            pltpu.VMEM((keys, wide), jnp.bfloat16),
            pltpu.VMEM((per, rows, each), jnp.bfloat16),
            pltpu.VMEM((per, rows, each), jnp.float32),
            pltpu.SMEM((1,), jnp.int32),
            pltpu.SMEM((pl.cdiv(pairs, BUNDLE) * BUNDLE,), jnp.int32),
            pltpu.SemaphoreType.DMA((2 * per,)),
        ],
        input_output_aliases=aliases,
        compiler_params=pltpu.CompilerParams(vmem_limit_bytes=(32 if pairs <= BUNDLE else 48) << 20),
        cost_estimate=pl.CostEstimate(flops=4 * macs, bytes_accessed=8 << 20, transcendentals=0),
    )(*args)


def add_kernel(mine_ref, got_ref, theirs_ref, last_ref, first_ref, *sends):
    first_ref[...] = (theirs_ref[0] + last_ref[0].astype(jnp.float32)).astype(jnp.bfloat16)
    for k, send in enumerate(sends):
        send[...] = (mine_ref[k] + got_ref[k].astype(jnp.float32)).astype(jnp.bfloat16)


def add_lanes(mine, got, theirs, last):
    count, tall, _ = mine.shape
    return pl.pallas_call(
        add_kernel,
        out_shape=[jax.ShapeDtypeStruct((tall, D), jnp.bfloat16)] * (count + 1),
        cost_estimate=pl.CostEstimate(flops=mine.size, bytes_accessed=8 * mine.size, transcendentals=0),
        compiler_params=pltpu.CompilerParams(vmem_limit_bytes=48 << 20),
    )(mine, got, theirs, last)


def finish_kernel(pairs, *refs):
    ins, (gk_ref, gv_ref) = refs[:-2], refs[-2:]
    rows = gk_ref.shape[1]
    each = pairs + 1
    per = ins[0].shape[1] // (2 * rows)
    for c in range(len(ins) // each):
        mine, last, *others = ins[c * each : (c + 1) * each]
        for g in range(per):
            cols = slice((c * per + g) * D, (c * per + g + 1) * D)
            for part, out in enumerate((gk_ref, gv_ref)):
                span = slice((2 * g + part) * rows, (2 * g + part + 1) * rows)
                total = mine[0, span, :] + last[0, span, :].astype(jnp.float32)
                for ref in others:
                    total = total + ref[span, :].astype(jnp.float32)
                out[0, :, cols] = total


def per_device(size, queries, key_matrix, value_matrix, cotangent, segment):
    rows = queries.shape[1]
    pairs = size // 2
    per = KV // CHUNKS
    here = lax.axis_index("ctx").astype(jnp.int32).reshape(1)

    def up(x, k):
        return lax.ppermute(x, "ctx", [(i, i + 2 * k) for i in range(size - 2 * k)])

    def down(x, k):
        return lax.ppermute(x, "ctx", [(i + 2 * k, i) for i in range(size - 2 * k)])

    def swap(x):
        return lax.ppermute(x, "ctx", [(i, i ^ 1) for i in range(size)])

    packed = pl.pallas_call(
        pack_kernel,
        out_shape=[jax.ShapeDtypeStruct((per * 2 * rows + 16, D), jnp.bfloat16)] * CHUNKS,
    )(key_matrix, value_matrix, segment)

    prev = None
    finals = []
    for c in range(CHUNKS):
        block = packed[c]
        own = [block] + [up(block, k) for k in range(1, pairs)]
        other = swap(block)
        peer = [other] + [swap(x) for x in own[1:-1]] + [up(other, pairs - 1)]
        attended, grad_query, mine_0, theirs_0, mine_mid, theirs_mid, mine_last, theirs_last = attend(
            c, here, own, peer, queries, cotangent, segment, prev
        )
        prev = (attended, grad_query)
        first, *mids = add_lanes(
            mine_mid, swap(theirs_mid), theirs_0, down(theirs_last, pairs - 1)
        )
        finals += [mine_0, down(mine_last, pairs - 1), swap(first)]
        finals += [down(x, k) for k, x in enumerate(mids, 1)]
    grads = pl.pallas_call(
        functools.partial(finish_kernel, pairs),
        out_shape=[jax.ShapeDtypeStruct(key_matrix.shape, jnp.float32)] * 2,
    )(*finals)
    return (attended, grad_query, grads[0], grads[1])


def solution(mesh):
    wide = P(("groups", "dp"), "ctx", None)
    return jax.shard_map(
        functools.partial(per_device, mesh.shape["ctx"]),
        mesh=mesh,
        in_specs=(wide, wide, wide, wide, P(("groups", "dp"), "ctx")),
        out_specs=(wide, wide, wide, wide),
        check_vma=False,
    )
```

```python
import functools
import math

import jax
import jax.numpy as jnp
from jax import lax
from jax.experimental import pallas as pl
from jax.experimental.pallas import tpu as pltpu
from jax.sharding import PartitionSpec as P

KV = 4
D = 128
SPLIT = (2, 2)
WORK = (((0, 2),), ((0, 2),))
VMEM = pl.BlockSpec(memory_space=pltpu.VMEM)
HBM = pl.BlockSpec(memory_space=pl.ANY)
BUNDLE = 4
LANES = 256
STEPS = 4
ROUND = True
NEG = -1e30
TIE1 = 2
TIE2 = True
FETCH = True
FULL = 57
FWD = True
NN = (((1,), (0,)), ((), ()))
NT = (((1,), (1,)), ((), ()))
TN = (((0,), (0,)), ((), ()))


def dot(a, b, dims):
    return lax.dot_general(a, b, dims, preferred_element_type=jnp.float32)


def pack_kernel(begin, per, k_ref, v_ref, s_ref, out, seg, sems):
    rows = k_ref.shape[1]
    copies = [pltpu.make_async_copy(s_ref, seg, sems.at[0])]
    for g in range(per):
        for part, ref in enumerate((k_ref, v_ref)):
            src = ref.at[0, :, pl.ds((begin + g) * D, D)]
            to = out.at[pl.ds((2 * g + part) * rows, rows)]
            copies.append(pltpu.make_async_copy(src, to, sems.at[1 + 2 * g + part]))
    for copy in copies:
        copy.start()
    for copy in copies:
        copy.wait()
    row = jnp.broadcast_to(seg[...].astype(jnp.float32), (16, rows))
    out[2 * per * rows :, :] = row.astype(jnp.bfloat16)


def pack(begin, per, key_matrix, value_matrix, segment):
    rows = key_matrix.shape[1]
    return pl.pallas_call(
        functools.partial(pack_kernel, begin, per),
        in_specs=[HBM] * 3,
        out_specs=VMEM,
        out_shape=jax.ShapeDtypeStruct((per * 2 * rows + 16, D), jnp.bfloat16),
        scratch_shapes=[
            pltpu.VMEM(segment.shape, jnp.int32),
            pltpu.SemaphoreType.DMA((2 * per + 1,)),
        ],
        compiler_params=pltpu.CompilerParams(vmem_limit_bytes=FULL << 20),
    )(key_matrix, value_matrix, segment)


def fetch_kernel(q_ref, c_ref, after_ref, q_out, c_out, sems):
    copies = [pltpu.make_async_copy(q_ref, q_out, sems.at[0]), pltpu.make_async_copy(c_ref, c_out, sems.at[1])]
    for copy in copies:
        copy.start()
    for copy in copies:
        copy.wait()


def fetch(queries, cotangent, after):
    return pl.pallas_call(
        fetch_kernel,
        in_specs=[HBM, HBM, HBM],
        out_specs=[VMEM, VMEM],
        out_shape=[jax.ShapeDtypeStruct(queries.shape, queries.dtype)] * 2,
        scratch_shapes=[pltpu.SemaphoreType.DMA((2,))],
        compiler_params=pltpu.CompilerParams(vmem_limit_bytes=16 << 20),
    )(queries, cotangent, after)


def loop(count, body, start, pairs):
    if pairs <= BUNDLE:
        return body(0, start)
    return lax.fori_loop(0, count, body, start)


def attend_kernel(pairs, begin, per, span_of_heads, lanes, prevs, here_ref, *refs):
    own = refs[:pairs]
    peer = refs[pairs : 2 * pairs]
    q_ref, c_ref, sq_ref = refs[2 * pairs : 2 * pairs + 3]
    refs = refs[2 * pairs + 3 + prevs :]
    low, high = span_of_heads
    out_ref, gq_ref = refs[:2]
    parts = refs[2:7]
    kv, mask, s_scr, p_scr, e_scr, probs_scr, slopes_scr, out_scr, gq_scr = refs[7:-3]
    cnt, order, sems = refs[-3:]
    rows = q_ref.shape[1]
    heads = q_ref.shape[2] // KV // D
    each = heads * D
    static = pairs <= BUNDLE
    wide = heads * rows
    two = 2 * rows
    tall = BUNDLE * two
    scale = 1.0 / math.sqrt(D)
    power = scale * math.log2(math.e)
    here = here_ref[0]

    def columns(g):
        return pl.ds((begin + low + g) * each, each)

    seg_q = sq_ref[...].astype(jnp.float32)
    q_pos = here * rows + lax.broadcasted_iota(jnp.int32, (rows, rows), 1)
    local = lax.broadcasted_iota(jnp.int32, (rows, rows), 0)
    sources = [src for k in range(pairs) for src in (own[k], peer[k])]
    base = 2 * per * rows
    seg_rows = [src[base : base + 16, :].astype(jnp.float32)[:1] for src in sources]
    seg_rows.append(jnp.zeros((rows - len(sources), rows), jnp.float32))
    seg_cols = jnp.transpose(jnp.concatenate(seg_rows, axis=0))

    def masks(k):
        adds = []
        for lane in range(2):
            block = (here ^ lane) - 2 * k
            seg_k = seg_cols[:, 2 * k + lane : 2 * k + lane + 1]
            ok = (block * rows + local <= q_pos) & ((seg_k == seg_q) | (seg_k == 0.0)) & (block >= 0)
            adds.append(jnp.where(ok, 0.0, NEG))
        return adds

    def store(at, k, adds):
        for lane, src in enumerate((own[k], peer[k])):
            to = pl.ds(pl.multiple_of(at + lane * rows, rows), rows)
            mask[to, :] = adds[lane]
            for h in range(low, high):
                for part in range(2):
                    kv[h - low, part, to, :] = src[(2 * h + part) * rows : (2 * h + part + 1) * rows, :]

    if static:
        for k in range(pairs):
            store(k * two, k, masks(k))
    else:
        cnt[0] = 0
        for k in range(pairs):
            adds = masks(k)

            @pl.when(jnp.max(jnp.maximum(adds[0], adds[1])) == 0.0)
            def _():
                store(cnt[0] * two, k, adds)
                order[cnt[0]] = k
                cnt[0] = cnt[0] + 1

        def blank(t, carry):
            at = pl.ds(pl.multiple_of(t * two, two), two)
            mask[at, :] = jnp.full((two, rows), NEG, jnp.float32)
            kv[:, :, at, :] = jnp.zeros((high - low, 2, two, D), jnp.bfloat16)
            order[t] = -1
            return carry

        lax.fori_loop(cnt[0], pl.cdiv(cnt[0], BUNDLE) * BUNDLE, blank, 0)
        for ref in parts:
            wipe = slice(low * two, high * two)
            ref[:, wipe, :] = jnp.zeros((ref.shape[0], (high - low) * two, D), ref.dtype)
    bundles = None if static else pl.cdiv(cnt[0], BUNDLE)
    copies = []

    def send(src, ref, g, which):
        copy = pltpu.make_async_copy(src.at[g], ref.at[0, :, columns(g)], sems.at[2 * g + which])
        copy.start()
        copies.append(copy)

    def stack(ref, g):
        first = (begin + low + g) * heads
        return jnp.concatenate([ref[0, :, (first + h) * D : (first + h + 1) * D] for h in range(heads)], axis=0)

    def tile(t, j):
        step = tall // STEPS
        return pl.ds(pl.multiple_of(t * tall + j * step, step), step)

    def span_of(t):
        return pl.ds(pl.multiple_of(t * tall, tall), tall)

    def one_head(g):
        q_all = stack(q_ref, g)
        c_all = stack(c_ref, g)
        at = (low + g) * two
        for w in range(wide // lanes):
            cols = slice(w * lanes, (w + 1) * lanes)
            q_w, c_w = q_all[cols], c_all[cols]

            def scores(t, top, q_w=q_w, c_w=c_w):
                span = span_of(t)
                s = dot(kv[g, 0, span, :], q_w, NT)
                s = s + jnp.concatenate([mask[span, :]] * (lanes // rows), axis=1)
                s_scr[span, :] = s
                p_scr[span, :] = dot(kv[g, 1, span, :], c_w, NT)
                top = jnp.maximum(top, jnp.max(s, axis=0, keepdims=True))
                return top

            top = loop(bundles, scores, jnp.full((1, lanes), NEG, jnp.float32), pairs)

            def forward(t, carry, top=top):
                total, delta, acc = carry
                for j in range(STEPS):
                    at = tile(t, j)
                    e = jnp.exp2((s_scr[at, :] - top) * power)
                    s_scr[at, :] = e
                    e_scr[at, :] = e.astype(jnp.bfloat16)
                    total = total + jnp.sum(e, axis=0, keepdims=True)
                    delta = delta + jnp.sum(e * p_scr[at, :], axis=0, keepdims=True)
                span = span_of(t)
                return total, delta, acc + dot(kv[g, 1, span, :], e_scr[span, :], TN)

            row = jnp.zeros((1, lanes), jnp.float32)
            total, delta, acc = loop(bundles, forward, (row, row, jnp.zeros((D, lanes), jnp.float32)), pairs)
            inverse = 1.0 / total
            delta = delta * inverse
            acc = acc * inverse
            for h in range(lanes // rows):
                to = slice((w * lanes // rows + h) * D, (w * lanes // rows + h + 1) * D)
                out_scr[g, :, to] = jnp.transpose(acc[:, h * rows : (h + 1) * rows]).astype(jnp.bfloat16)

            def backward(t, acc, inverse=inverse, delta=delta, cols=cols):
                for j in range(STEPS):
                    at = tile(t, j)
                    probs = s_scr[at, :] * inverse
                    probs_scr[at, cols] = probs.astype(jnp.bfloat16)
                    slopes_scr[at, cols] = (probs * (p_scr[at, :] - delta)).astype(jnp.bfloat16)
                span = span_of(t)
                return acc + dot(kv[g, 0, span, :], slopes_scr[span, cols], TN)

            grad = loop(bundles, backward, jnp.zeros((D, lanes), jnp.float32), pairs) * scale
            for h in range(lanes // rows):
                to = slice((w * lanes // rows + h) * D, (w * lanes // rows + h + 1) * D)
                gq_scr[g, :, to] = jnp.transpose(grad[:, h * rows : (h + 1) * rows])

        send(out_scr, out_ref, g, 0)
        send(gq_scr, gq_ref, g, 1)

        def key_side(t, carry):
            span = span_of(t)
            all_v = dot(probs_scr[span, :], c_all, NN)
            all_k = dot(slopes_scr[span, :], q_all, NN) * scale
            for j in range(BUNDLE):
                k = None if static else order[t * BUNDLE + j]
                grad_v = all_v[j * two : (j + 1) * two]
                grad_k = all_k[j * two : (j + 1) * two]

                def keep(first, slot):
                    for lane in range(2):
                        ref = parts[min(first + lane, 4)]
                        slot = lane if first == 4 else slot
                        part = slice(lane * rows, (lane + 1) * rows)
                        ref[slot, pl.ds(at, rows), :] = grad_k[part].astype(ref.dtype)
                        ref[slot, pl.ds(at + rows, rows), :] = grad_v[part].astype(ref.dtype)

                if static:
                    keep(*((0, 0) if j == 0 else (4, 0) if j == pairs - 1 else (2, j - 1)))
                    continue
                pl.when(k == 0)(lambda: keep(0, 0))
                pl.when((k > 0) & (k < pairs - 1))(lambda: keep(2, k - 1))
                pl.when(k == pairs - 1)(lambda: keep(4, 0))
            return carry

        loop(bundles, key_side, 0, pairs)

    for g in range(high - low):
        one_head(g)
    for copy in copies:
        copy.wait()


def attend(begin, per, heads, here, own, peer, queries, cotangent, segment, prev, made):
    pairs = len(own)
    count = heads[1] - heads[0]
    _, rows, width = queries.shape
    each = width // KV
    wide = each // D * rows
    lanes = wide if pairs <= BUNDLE else LANES
    keys = pl.cdiv(pairs, BUNDLE) * BUNDLE * 2 * rows
    parts = [
        jax.ShapeDtypeStruct((count, per * 2 * rows, D), dtype)
        for count, dtype in (
            (1, jnp.float32),
            (1, jnp.float32),
            (pairs - 2, jnp.float32),
            (pairs - 2, jnp.bfloat16),
            (2, jnp.bfloat16),
        )
    ]
    args = [here, *own, *peer, queries, cotangent, segment]
    in_specs = [pl.BlockSpec(memory_space=pltpu.SMEM)] + [VMEM] * (2 * pairs) + [VMEM] * 3
    aliases = {}
    if prev is not None:
        aliases.update({len(args): 0, len(args) + 1: 1})
        args += list(prev)
        in_specs += [HBM] * 2
    if made is not None:
        aliases.update({len(args) + i: 2 + i for i in range(len(made))})
        args += list(made)
        in_specs += [VMEM] * len(made)
    macs = count * wide * 2 * rows * D * 6 * pairs
    return pl.pallas_call(
        functools.partial(attend_kernel, pairs, begin, per, heads, lanes, len(args) - 2 * pairs - 4),
        in_specs=in_specs,
        out_specs=[HBM, HBM] + [VMEM] * len(parts),
        out_shape=[
            jax.ShapeDtypeStruct(queries.shape, jnp.bfloat16),
            jax.ShapeDtypeStruct(queries.shape, jnp.float32),
            *parts,
        ],
        scratch_shapes=[
            pltpu.VMEM((count, 2, keys, D), jnp.bfloat16),
            pltpu.VMEM((keys, rows), jnp.float32),
            pltpu.VMEM((keys, lanes), jnp.float32),
            pltpu.VMEM((keys, lanes), jnp.float32),
            pltpu.VMEM((keys, lanes), jnp.bfloat16),
            pltpu.VMEM((keys, wide), jnp.bfloat16),
            pltpu.VMEM((keys, wide), jnp.bfloat16),
            pltpu.VMEM((count, rows, each), jnp.bfloat16),
            pltpu.VMEM((count, rows, each), jnp.float32),
            pltpu.SMEM((1,), jnp.int32),
            pltpu.SMEM((pl.cdiv(pairs, BUNDLE) * BUNDLE,), jnp.int32),
            pltpu.SemaphoreType.DMA((2 * count,)),
        ],
        input_output_aliases=aliases,
        compiler_params=pltpu.CompilerParams(vmem_limit_bytes=(32 if pairs <= BUNDLE else 48) << 20),
        cost_estimate=pl.CostEstimate(flops=4 * macs, bytes_accessed=8 << 20, transcendentals=0),
    )(*args)


def add_kernel(mine_ref, got_ref, theirs_ref, last_ref, first_ref, *sends):
    first_ref[...] = (theirs_ref[0] + last_ref[1].astype(jnp.float32)).astype(jnp.bfloat16)
    for k, send in enumerate(sends):
        send[...] = (mine_ref[k] + got_ref[k].astype(jnp.float32)).astype(jnp.bfloat16)


def add_lanes(mine, got, theirs, last):
    count, tall, _ = mine.shape
    return pl.pallas_call(
        add_kernel,
        in_specs=[VMEM] * 4,
        out_specs=[VMEM] * (count + 1),
        out_shape=[jax.ShapeDtypeStruct((tall, D), jnp.bfloat16)] * (count + 1),
        cost_estimate=pl.CostEstimate(flops=mine.size, bytes_accessed=8 * mine.size, transcendentals=0),
        compiler_params=pltpu.CompilerParams(vmem_limit_bytes=48 << 20),
    )(mine, got, theirs, last)


def finish_kernel(pairs, *refs):
    ins, (gk_ref, gv_ref) = refs[:-2], refs[-2:]
    rows = gk_ref.shape[1]
    each = pairs + 1
    head = 0
    for c in range(len(ins) // each):
        mine, last, *others = ins[c * each : (c + 1) * each]
        for g in range(mine.shape[1] // (2 * rows)):
            cols = slice(head * D, (head + 1) * D)
            head += 1
            for part, out in enumerate((gk_ref, gv_ref)):
                span = slice((2 * g + part) * rows, (2 * g + part + 1) * rows)
                total = mine[0, span, :] + last[0, span, :].astype(jnp.float32)
                for ref in others:
                    total = total + ref[span, :].astype(jnp.float32)
                out[0, :, cols] = total


def per_device(size, queries, key_matrix, value_matrix, cotangent, segment):
    rows = queries.shape[1]
    pairs = size // 2
    here = lax.axis_index("ctx").astype(jnp.int32).reshape(1)

    def up(x, k):
        return lax.ppermute(x, "ctx", [(i, (i + 2 * k) % size) for i in range(size if ROUND else size - 2 * k)])

    def down(x, k):
        return lax.ppermute(x, "ctx", [((i + 2 * k) % size, i) for i in range(size if ROUND else size - 2 * k)])

    def swap(x):
        return lax.ppermute(x, "ctx", [(i, i ^ 1) for i in range(size)])

    def far(block):
        if not FWD:
            return [swap(block)] + [up(block, k) for k in range(1, pairs)]
        own = [block]
        for _ in range(pairs - 2):
            own.append(up(own[-1], 1))
        return [swap(block), *own[1:], up(block, pairs - 1)]

    def near(block, first):
        other, *mids, top = first
        return [block, *mids, top], [other, *(swap(x) for x in mids), up(other, pairs - 1)]

    finals = []
    blocks = []
    begin = 0
    for per in SPLIT:
        blocks.append(pack(begin, per, key_matrix, value_matrix, segment))
        begin += per
    begin = 0
    prev = None
    first = far(blocks[0])
    if FETCH:
        queries, cotangent = fetch(queries, cotangent, blocks[0])
    def later(values, event):
        return lax.optimization_barrier((*values, event))[:-1]

    waiting = None

    def finish(waiting):
        mine_0, theirs_0, mine_mid, got, last = waiting
        lower, *mids = add_lanes(mine_mid, got, theirs_0, last)
        downs = [down(x, k) for k, x in enumerate(mids, 1)]
        finals.extend([mine_0, last, swap(lower), *downs])

    if FETCH:
        first[1], queries, cotangent = lax.optimization_barrier((first[1], queries, cotangent))
    for c, per in enumerate(SPLIT):
        more = c + 1 < len(SPLIT)
        own, peer = near(blocks[c], first)
        if more:
            (block,) = later(blocks[c + 1 : c + 2], own[TIE1])
            blocks[c + 1] = block
            first = far(block)
        made = None
        for step, heads in enumerate(WORK[c]):
            attended, grad_query, *made = attend(
                begin, per, heads, here, own, peer, queries, cotangent, segment, prev, made
            )
            prev = (attended, grad_query)
            if step == 0 and waiting is not None:
                waiting[3], waiting[4] = later(waiting[3:], made[0])
                finish(waiting)
                waiting = None
            if step == 0 and more and TIE2:
                first = list(later(first, made[0]))
        begin += per
        mine_0, theirs_0, mine_mid, theirs_mid, last = made
        waiting = [mine_0, theirs_0, mine_mid, swap(theirs_mid), down(last, pairs - 1)]
    finish(waiting)
    grads = pl.pallas_call(
        functools.partial(finish_kernel, pairs),
        in_specs=[VMEM] * len(finals),
        out_specs=[VMEM] * 2,
        compiler_params=pltpu.CompilerParams(vmem_limit_bytes=16 << 20),
        out_shape=[jax.ShapeDtypeStruct(key_matrix.shape, jnp.float32)] * 2,
    )(*finals)
    return (attended, grad_query, grads[0], grads[1])


def solution(mesh):
    wide = P(("groups", "dp"), "ctx", None)
    return jax.shard_map(
        functools.partial(per_device, mesh.shape["ctx"]),
        mesh=mesh,
        in_specs=(wide, wide, wide, wide, P(("groups", "dp"), "ctx")),
        out_specs=(wide, wide, wide, wide),
        check_vma=False,
    )
```

```python
import functools
import math

import jax
import jax.numpy as jnp
from jax import lax
from jax.experimental import pallas as pl
from jax.experimental.pallas import tpu as pltpu
from jax.sharding import PartitionSpec as P

KV = 4
D = 128
SPLIT = (2, 2)
WORK = (((0, 2),), ((0, 2),))
VMEM = pl.BlockSpec(memory_space=pltpu.VMEM)
HBM = pl.BlockSpec(memory_space=pl.ANY)
BUNDLE = 4
LANES = 256
STEPS = 1
MIX = True
ROUND = True
NEG = -1e30
TIE1 = 5
TIE2 = True
DIRECT = True
FULL = 57
NN = (((1,), (0,)), ((), ()))
NT = (((1,), (1,)), ((), ()))
TN = (((0,), (0,)), ((), ()))


def dot(a, b, dims):
    return lax.dot_general(a, b, dims, preferred_element_type=jnp.float32)


def pack_kernel(begin, per, k_ref, v_ref, s_ref, out, seg, sems):
    rows = k_ref.shape[1]
    copies = [pltpu.make_async_copy(s_ref, seg, sems.at[0])]
    for g in range(per):
        for part, ref in enumerate((k_ref, v_ref)):
            src = ref.at[0, :, pl.ds((begin + g) * D, D)]
            to = out.at[pl.ds((2 * g + part) * rows, rows)]
            copies.append(pltpu.make_async_copy(src, to, sems.at[1 + 2 * g + part]))
    for copy in copies:
        copy.start()
    for copy in copies:
        copy.wait()
    row = jnp.broadcast_to(seg[...].astype(jnp.float32), (16, rows))
    out[2 * per * rows :, :] = row.astype(jnp.bfloat16)


def pack(begin, per, key_matrix, value_matrix, segment):
    rows = key_matrix.shape[1]
    return pl.pallas_call(
        functools.partial(pack_kernel, begin, per),
        in_specs=[HBM] * 3,
        out_specs=VMEM,
        out_shape=jax.ShapeDtypeStruct((per * 2 * rows + 16, D), jnp.bfloat16),
        scratch_shapes=[
            pltpu.VMEM(segment.shape, jnp.int32),
            pltpu.SemaphoreType.DMA((2 * per + 1,)),
        ],
        compiler_params=pltpu.CompilerParams(vmem_limit_bytes=FULL << 20),
    )(key_matrix, value_matrix, segment)


def fetch_kernel(q_ref, c_ref, after_ref, q_out, c_out, sems):
    copies = [pltpu.make_async_copy(q_ref, q_out, sems.at[0]), pltpu.make_async_copy(c_ref, c_out, sems.at[1])]
    for copy in copies:
        copy.start()
    for copy in copies:
        copy.wait()


def fetch(queries, cotangent, after):
    return pl.pallas_call(
        fetch_kernel,
        in_specs=[HBM, HBM, HBM],
        out_specs=[VMEM, VMEM],
        out_shape=[jax.ShapeDtypeStruct(queries.shape, queries.dtype)] * 2,
        scratch_shapes=[pltpu.SemaphoreType.DMA((2,))],
        compiler_params=pltpu.CompilerParams(vmem_limit_bytes=16 << 20),
    )(queries, cotangent, after)


def loop(count, body, start, pairs):
    if pairs <= BUNDLE:
        return body(0, start)
    return lax.fori_loop(0, count, body, start)


def attend_kernel(pairs, begin, per, span_of_heads, lanes, prevs, here_ref, *refs):
    own = refs[:pairs]
    peer = refs[pairs : 2 * pairs]
    q_ref, c_ref, sq_ref = refs[2 * pairs : 2 * pairs + 3]
    refs = refs[2 * pairs + 3 + prevs :]
    low, high = span_of_heads
    out_ref, gq_ref = refs[:2]
    parts = refs[2:7]
    kv, mask, s_scr, p_scr, e_scr, probs_scr, slopes_scr, out_scr, gq_scr = refs[7:-3]
    cnt, order, sems = refs[-3:]
    rows = q_ref.shape[1]
    heads = q_ref.shape[2] // KV // D
    each = heads * D
    static = pairs <= BUNDLE
    wide = heads * rows
    two = 2 * rows
    tall = BUNDLE * two
    keys = mask.shape[0]
    scale = 1.0 / math.sqrt(D)
    power = scale * math.log2(math.e)
    here = here_ref[0]

    def columns(g):
        return pl.ds((begin + low + g) * each, each)

    seg_q = sq_ref[...].astype(jnp.float32)
    q_pos = here * rows + lax.broadcasted_iota(jnp.int32, (rows, rows), 1)
    local = lax.broadcasted_iota(jnp.int32, (rows, rows), 0)
    sources = [src for k in range(pairs) for src in (own[k], peer[k])]
    base = 2 * per * rows
    seg_rows = [src[base : base + 16, :].astype(jnp.float32)[:1] for src in sources]
    seg_rows.append(jnp.zeros((rows - len(sources), rows), jnp.float32))
    seg_cols = jnp.transpose(jnp.concatenate(seg_rows, axis=0))

    def masks(k):
        adds = []
        for lane in range(2):
            block = (here ^ lane) - 2 * k
            seg_k = seg_cols[:, 2 * k + lane : 2 * k + lane + 1]
            ok = (block * rows + local <= q_pos) & ((seg_k == seg_q) | (seg_k == 0.0)) & (block >= 0)
            adds.append(jnp.where(ok, 0.0, NEG))
        return adds

    def store(at, k, adds):
        for lane, src in enumerate((own[k], peer[k])):
            to = pl.ds(pl.multiple_of(at + lane * rows, rows), rows)
            mask[to, :] = adds[lane]
            for h in range(low, high):
                for part in range(2):
                    kv[h - low, part, to, :] = src[(2 * h + part) * rows : (2 * h + part + 1) * rows, :]

    if static:
        for k in range(pairs):
            store(k * two, k, masks(k))
    else:
        cnt[0] = 0
        for k in range(pairs):
            adds = masks(k)

            @pl.when(jnp.max(jnp.maximum(adds[0], adds[1])) == 0.0)
            def _():
                store(cnt[0] * two, k, adds)
                order[cnt[0]] = k
                cnt[0] = cnt[0] + 1

        def blank(t, carry):
            at = pl.ds(pl.multiple_of(t * two, two), two)
            mask[at, :] = jnp.full((two, rows), NEG, jnp.float32)
            kv[:, :, at, :] = jnp.zeros((high - low, 2, two, D), jnp.bfloat16)
            order[t] = -1
            return carry

        lax.fori_loop(cnt[0], pl.cdiv(cnt[0], BUNDLE) * BUNDLE, blank, 0)
        for ref in parts:
            wipe = slice(low * two, high * two)
            ref[:, wipe, :] = jnp.zeros((ref.shape[0], (high - low) * two, D), ref.dtype)
    bundles = None if static else pl.cdiv(cnt[0], BUNDLE)
    copies = []

    def send(src, ref, g, which):
        copy = pltpu.make_async_copy(src.at[g], ref.at[0, :, columns(g)], sems.at[2 * g + which])
        copy.start()
        copies.append(copy)

    def stack(ref, g):
        first = (begin + low + g) * heads
        return jnp.concatenate([ref[0, :, (first + h) * D : (first + h + 1) * D] for h in range(heads)], axis=0)

    def tile(t, j):
        step = tall // STEPS
        return pl.ds(pl.multiple_of(t * tall + j * step, step), step)

    def span_of(t):
        return pl.ds(pl.multiple_of(t * tall, tall), tall)

    def one_head(g):
        q_all = stack(q_ref, g)
        c_all = stack(c_ref, g)
        at = (low + g) * two
        for w in range(wide // lanes):
            cols = slice(w * lanes, (w + 1) * lanes)
            q_w, c_w = q_all[cols], c_all[cols]

            def scores(t, top, q_w=q_w, c_w=c_w):
                span = span_of(t)
                s = dot(kv[g, 0, span, :], q_w, NT)
                s = s + jnp.concatenate([mask[span, :]] * (lanes // rows), axis=1)
                s_scr[span, :] = s
                p_scr[span, :] = dot(kv[g, 1, span, :], c_w, NT)
                top = jnp.maximum(top, jnp.max(s, axis=0, keepdims=True))
                return top

            top = loop(bundles, scores, jnp.full((1, lanes), NEG, jnp.float32), pairs)

            def forward(t, carry, top=top):
                total, delta, acc = carry
                for j in range(STEPS):
                    at = tile(t, j)
                    e = jnp.exp2((s_scr[at, :] - top) * power)
                    s_scr[at, :] = e
                    e_scr[at, :] = e.astype(jnp.bfloat16)
                    total = total + jnp.sum(e, axis=0, keepdims=True)
                    delta = delta + jnp.sum(e * p_scr[at, :], axis=0, keepdims=True)
                span = span_of(t)
                return total, delta, acc + dot(kv[g, 1, span, :], e_scr[span, :], TN)

            row = jnp.zeros((1, lanes), jnp.float32)
            total, delta, acc = loop(bundles, forward, (row, row, jnp.zeros((D, lanes), jnp.float32)), pairs)
            inverse = 1.0 / total
            delta = delta * inverse
            acc = acc * inverse
            for h in range(lanes // rows):
                to = slice((w * lanes // rows + h) * D, (w * lanes // rows + h + 1) * D)
                out_scr[g, :, to] = jnp.transpose(acc[:, h * rows : (h + 1) * rows]).astype(jnp.bfloat16)

            def backward(t, acc, inverse=inverse, delta=delta, cols=cols):
                for j in range(STEPS):
                    at = tile(t, j)
                    probs = s_scr[at, :] * inverse
                    probs_scr[at, cols] = probs.astype(jnp.bfloat16)
                    slopes_scr[at, cols] = (probs * (p_scr[at, :] - delta)).astype(jnp.bfloat16)
                span = span_of(t)
                return acc + dot(kv[g, 0, span, :], slopes_scr[span, cols], TN)

            grad = loop(bundles, backward, jnp.zeros((D, lanes), jnp.float32), pairs) * scale
            for h in range(lanes // rows):
                to = slice((w * lanes // rows + h) * D, (w * lanes // rows + h + 1) * D)
                gq_scr[g, :, to] = jnp.transpose(grad[:, h * rows : (h + 1) * rows])

        send(out_scr, out_ref, g, 0)
        send(gq_scr, gq_ref, g, 1)

        def key_side(t, carry):
            span = span_of(t)
            all_v = dot(probs_scr[span, :], c_all, NN)
            all_k = dot(slopes_scr[span, :], q_all, NN) * scale
            for j in range(BUNDLE):
                k = None if static else order[t * BUNDLE + j]
                grad_v = all_v[j * two : (j + 1) * two]
                grad_k = all_k[j * two : (j + 1) * two]

                def keep(first, slot):
                    for lane in range(2):
                        ref = parts[min(first + lane, 4)]
                        slot = lane if first == 4 else slot
                        part = slice(lane * rows, (lane + 1) * rows)
                        ref[slot, pl.ds(at, rows), :] = grad_k[part].astype(ref.dtype)
                        ref[slot, pl.ds(at + rows, rows), :] = grad_v[part].astype(ref.dtype)

                if static:
                    keep(*((0, 0) if j == 0 else (4, 0) if j == pairs - 1 else (2, j - 1)))
                    continue
                pl.when(k == 0)(lambda: keep(0, 0))
                pl.when((k > 0) & (k < pairs - 1))(lambda: keep(2, k - 1))
                pl.when(k == pairs - 1)(lambda: keep(4, 0))
            return carry

        loop(bundles, key_side, 0, pairs)

    def interleaved(count):
        state = [{} for _ in range(count)]
        steps = range(STEPS)

        def offset(g):
            return g * keys

        def rows_of(g, j):
            step = keys // STEPS
            return slice(offset(g) + j * step, offset(g) + (j + 1) * step)

        def score(g, j):
            st = state[g]
            if j == 0:
                st["q"], st["c"] = stack(q_ref, g), stack(c_ref, g)
                st["top"] = jnp.full((1, wide), NEG, jnp.float32)
            at, to = tile(0, j), rows_of(g, j)
            s = dot(kv[g, 0, at, :], st["q"], NT)
            s = s + jnp.concatenate([mask[at, :]] * heads, axis=1)
            s_scr[to, :] = s
            p_scr[to, :] = dot(kv[g, 1, at, :], st["c"], NT)
            st["top"] = jnp.maximum(st["top"], jnp.max(s, axis=0, keepdims=True))

        def weigh(g, j):
            st, to = state[g], rows_of(g, j)
            e = jnp.exp2((s_scr[to, :] - st["top"]) * power)
            s_scr[to, :] = e
            e_scr[to, :] = e.astype(jnp.bfloat16)
            total = jnp.sum(e, axis=0, keepdims=True)
            delta = jnp.sum(e * p_scr[to, :], axis=0, keepdims=True)
            st["total"] = total if j == 0 else st["total"] + total
            st["delta"] = delta if j == 0 else st["delta"] + delta

        def outputs(g):
            st = state[g]
            st["inverse"] = 1.0 / st["total"]
            st["delta"] = st["delta"] * st["inverse"]
            acc = dot(kv[g, 1], e_scr[offset(g) : offset(g) + keys, :], TN) * st["inverse"]
            for h in range(heads):
                out = jnp.transpose(acc[:, h * rows : (h + 1) * rows])
                out_scr[g, :, h * D : (h + 1) * D] = out.astype(jnp.bfloat16)
            send(out_scr, out_ref, g, 0)

        def slope(g, j):
            st, to = state[g], rows_of(g, j)
            probs = s_scr[to, :] * st["inverse"]
            probs_scr[to, :] = probs.astype(jnp.bfloat16)
            slopes_scr[to, :] = (probs * (p_scr[to, :] - st["delta"])).astype(jnp.bfloat16)

        def query_side(g):
            grad = dot(kv[g, 0], slopes_scr[offset(g) : offset(g) + keys, :], TN) * scale
            for h in range(heads):
                gq_scr[g, :, h * D : (h + 1) * D] = jnp.transpose(grad[:, h * rows : (h + 1) * rows])
            send(gq_scr, gq_ref, g, 1)

        def key_side(g):
            st = state[g]
            span = slice(offset(g), offset(g) + keys)
            all_v = dot(probs_scr[span, :], st["c"], NN)
            all_k = dot(slopes_scr[span, :], st["q"], NN) * scale
            first = (low + g) * two
            for k in range(pairs):
                for lane in range(2):
                    base = 0 if k == 0 else 4 if k == pairs - 1 else 2
                    ref = parts[min(base + lane, 4)]
                    slot = 0 if k == 0 else lane if k == pairs - 1 else k - 1
                    part = slice(k * two + lane * rows, k * two + (lane + 1) * rows)
                    ref[slot, first : first + rows, :] = all_k[part].astype(ref.dtype)
                    ref[slot, first + rows : first + two, :] = all_v[part].astype(ref.dtype)

        for j in steps:
            score(0, j)
        for g in range(count):
            for j in steps:
                weigh(g, j)
                if g + 1 < count and MIX:
                    score(g + 1, j)
            outputs(g)
            for j in steps:
                slope(g, j)
            query_side(g)
            key_side(g)
            if g + 1 < count and not MIX:
                for j in steps:
                    score(g + 1, j)

    if static:
        interleaved(high - low)
    else:
        for g in range(high - low):
            one_head(g)
    for copy in copies:
        copy.wait()


def attend(begin, per, heads, here, own, peer, queries, cotangent, segment, prev, made):
    pairs = len(own)
    count = heads[1] - heads[0]
    _, rows, width = queries.shape
    each = width // KV
    wide = each // D * rows
    lanes = wide if pairs <= BUNDLE else LANES
    keys = pl.cdiv(pairs, BUNDLE) * BUNDLE * 2 * rows
    many = count if pairs <= BUNDLE else 1
    parts = [
        jax.ShapeDtypeStruct((count, per * 2 * rows, D), dtype)
        for count, dtype in (
            (1, jnp.float32),
            (1, jnp.float32),
            (pairs - 2, jnp.float32),
            (pairs - 2, jnp.bfloat16),
            (2, jnp.bfloat16),
        )
    ]
    args = [here, *own, *peer, queries, cotangent, segment]
    in_specs = [pl.BlockSpec(memory_space=pltpu.SMEM)] + [VMEM] * (2 * pairs) + [VMEM] * 3
    aliases = {}
    if prev is not None:
        aliases.update({len(args): 0, len(args) + 1: 1})
        args += list(prev)
        in_specs += [HBM] * 2
    if made is not None:
        aliases.update({len(args) + i: 2 + i for i in range(len(made))})
        args += list(made)
        in_specs += [VMEM] * len(made)
    macs = count * wide * 2 * rows * D * 6 * pairs
    return pl.pallas_call(
        functools.partial(attend_kernel, pairs, begin, per, heads, lanes, len(args) - 2 * pairs - 4),
        in_specs=in_specs,
        out_specs=[HBM, HBM] + [VMEM] * len(parts),
        out_shape=[
            jax.ShapeDtypeStruct(queries.shape, jnp.bfloat16),
            jax.ShapeDtypeStruct(queries.shape, jnp.float32),
            *parts,
        ],
        scratch_shapes=[
            pltpu.VMEM((count, 2, keys, D), jnp.bfloat16),
            pltpu.VMEM((keys, rows), jnp.float32),
            pltpu.VMEM((many * keys, lanes), jnp.float32),
            pltpu.VMEM((many * keys, lanes), jnp.float32),
            pltpu.VMEM((many * keys, lanes), jnp.bfloat16),
            pltpu.VMEM((many * keys, wide), jnp.bfloat16),
            pltpu.VMEM((many * keys, wide), jnp.bfloat16),
            pltpu.VMEM((count, rows, each), jnp.bfloat16),
            pltpu.VMEM((count, rows, each), jnp.float32),
            pltpu.SMEM((1,), jnp.int32),
            pltpu.SMEM((pl.cdiv(pairs, BUNDLE) * BUNDLE,), jnp.int32),
            pltpu.SemaphoreType.DMA((2 * count,)),
        ],
        input_output_aliases=aliases,
        compiler_params=pltpu.CompilerParams(vmem_limit_bytes=48 << 20),
        cost_estimate=pl.CostEstimate(flops=4 * macs, bytes_accessed=8 << 20, transcendentals=0),
    )(*args)


def add_kernel(mine_ref, got_ref, theirs_ref, last_ref, first_ref, *sends):
    first_ref[...] = (theirs_ref[0] + last_ref[1].astype(jnp.float32)).astype(jnp.bfloat16)
    for k, send in enumerate(sends):
        send[...] = (mine_ref[k] + got_ref[k].astype(jnp.float32)).astype(jnp.bfloat16)


def add_lanes(mine, got, theirs, last):
    count, tall, _ = mine.shape
    return pl.pallas_call(
        add_kernel,
        in_specs=[VMEM] * 4,
        out_specs=[VMEM] * (count + 1),
        out_shape=[jax.ShapeDtypeStruct((tall, D), jnp.bfloat16)] * (count + 1),
        cost_estimate=pl.CostEstimate(flops=mine.size, bytes_accessed=8 * mine.size, transcendentals=0),
        compiler_params=pltpu.CompilerParams(vmem_limit_bytes=48 << 20),
    )(mine, got, theirs, last)


def finish_kernel(pairs, *refs):
    ins, (gk_ref, gv_ref) = refs[:-2], refs[-2:]
    rows = gk_ref.shape[1]
    each = pairs + 1
    head = 0
    for c in range(len(ins) // each):
        mine, last, *others = ins[c * each : (c + 1) * each]
        for g in range(mine.shape[1] // (2 * rows)):
            cols = slice(head * D, (head + 1) * D)
            head += 1
            for part, out in enumerate((gk_ref, gv_ref)):
                span = slice((2 * g + part) * rows, (2 * g + part + 1) * rows)
                total = mine[0, span, :] + last[0, span, :].astype(jnp.float32)
                for ref in others:
                    total = total + ref[span, :].astype(jnp.float32)
                out[0, :, cols] = total


def per_device(size, queries, key_matrix, value_matrix, cotangent, segment):
    rows = queries.shape[1]
    pairs = size // 2
    here = lax.axis_index("ctx").astype(jnp.int32).reshape(1)

    def up(x, k):
        return lax.ppermute(x, "ctx", [(i, (i + 2 * k) % size) for i in range(size if ROUND else size - 2 * k)])

    def down(x, k):
        return lax.ppermute(x, "ctx", [((i + 2 * k) % size, i) for i in range(size if ROUND else size - 2 * k)])

    def swap(x):
        return lax.ppermute(x, "ctx", [(i, i ^ 1) for i in range(size)])

    def far(block, direct, meanwhile=()):
        own = [up(block, 1)]
        for k in range(2, pairs - 1):
            if direct:
                own.append(up(block, k))
                continue
            if k == 2 and meanwhile:
                own[0], *meanwhile = lax.optimization_barrier((own[0], *meanwhile))
            own.append(up(own[-1], 1))
        return [swap(block), *own, up(block, pairs - 1)], meanwhile

    def near(block, first):
        other, *mids, top = first
        return [block, *mids, top], [other, *(swap(x) for x in mids), up(other, pairs - 1)]

    finals = []
    blocks = []
    begin = 0
    for per in SPLIT:
        blocks.append(pack(begin, per, key_matrix, value_matrix, segment))
        begin += per
    begin = 0
    prev = None
    queries, cotangent = fetch(queries, cotangent, blocks[0])
    first, (queries, cotangent) = far(blocks[0], False, (queries, cotangent))

    def later(values, event):
        return lax.optimization_barrier((*values, event))[:-1]

    waiting = None

    def finish(waiting):
        mine_0, theirs_0, mine_mid, got, last = waiting
        lower, *mids = add_lanes(mine_mid, got, theirs_0, last)
        downs = [down(x, k) for k, x in enumerate(mids, 1)]
        finals.extend([mine_0, last, swap(lower), *downs])

    for c, per in enumerate(SPLIT):
        more = c + 1 < len(SPLIT)
        own, peer = near(blocks[c], first)
        if more:
            (block,) = later(blocks[c + 1 : c + 2], (own + peer)[TIE1])
            blocks[c + 1] = block
            first, _ = far(block, DIRECT)
        made = None
        for step, heads in enumerate(WORK[c]):
            attended, grad_query, *made = attend(
                begin, per, heads, here, own, peer, queries, cotangent, segment, prev, made
            )
            prev = (attended, grad_query)
            if step == 0 and waiting is not None:
                waiting[3], waiting[4] = later(waiting[3:], made[0])
                finish(waiting)
                waiting = None
            if step == 0 and more and TIE2:
                first = list(later(first, made[0]))
        begin += per
        mine_0, theirs_0, mine_mid, theirs_mid, last = made
        waiting = [mine_0, theirs_0, mine_mid, swap(theirs_mid), down(last, pairs - 1)]
    finish(waiting)
    grads = pl.pallas_call(
        functools.partial(finish_kernel, pairs),
        in_specs=[VMEM] * len(finals),
        out_specs=[VMEM] * 2,
        compiler_params=pltpu.CompilerParams(vmem_limit_bytes=16 << 20),
        out_shape=[jax.ShapeDtypeStruct(key_matrix.shape, jnp.float32)] * 2,
    )(*finals)
    return (attended, grad_query, grads[0], grads[1])


def solution(mesh):
    wide = P(("groups", "dp"), "ctx", None)
    return jax.shard_map(
        functools.partial(per_device, mesh.shape["ctx"]),
        mesh=mesh,
        in_specs=(wide, wide, wide, wide, P(("groups", "dp"), "ctx")),
        out_specs=(wide, wide, wide, wide),
        check_vma=False,
    )
```

```python
import functools
import math

import jax
import jax.numpy as jnp
from jax import lax
from jax.experimental import pallas as pl
from jax.experimental.pallas import tpu as pltpu
from jax.sharding import PartitionSpec as P

KV = 4
D = 128
SPLIT = (2, 2)
VMEM = pl.BlockSpec(memory_space=pltpu.VMEM)
HBM = pl.BlockSpec(memory_space=pl.ANY)
BUNDLE = 4
LANES = 256
STEPS = 1
ORDER = 0
ROUND = True
NEG = -1e30
TIE1 = 5
TIE2 = True
TIE3 = False
DIRECT = True
FULL = 57
NN = (((1,), (0,)), ((), ()))
NT = (((1,), (1,)), ((), ()))
TN = (((0,), (0,)), ((), ()))


def dot(a, b, dims):
    return lax.dot_general(a, b, dims, preferred_element_type=jnp.float32)


def pack_kernel(k_ref, v_ref, s_ref, *refs):
    *outs, seg, sems = refs
    rows = k_ref.shape[1]
    copies = [pltpu.make_async_copy(s_ref, seg, sems.at[0])]
    head = 0
    for per, out in zip(SPLIT, outs):
        for g in range(per):
            for part, ref in enumerate((k_ref, v_ref)):
                src = ref.at[0, :, pl.ds(head * D, D)]
                to = out.at[pl.ds((2 * g + part) * rows, rows)]
                copies.append(pltpu.make_async_copy(src, to, sems.at[1 + 2 * head + part]))
            head += 1
    for copy in copies:
        copy.start()
    for copy in copies:
        copy.wait()
    row = jnp.broadcast_to(seg[...].astype(jnp.float32), (16, rows)).astype(jnp.bfloat16)
    for per, out in zip(SPLIT, outs):
        out[2 * per * rows :, :] = row


def pack(key_matrix, value_matrix, segment):
    rows = key_matrix.shape[1]
    return pl.pallas_call(
        pack_kernel,
        in_specs=[HBM] * 3,
        out_specs=[VMEM] * len(SPLIT),
        out_shape=[jax.ShapeDtypeStruct((per * 2 * rows + 16, D), jnp.bfloat16) for per in SPLIT],
        scratch_shapes=[
            pltpu.VMEM(segment.shape, jnp.int32),
            pltpu.SemaphoreType.DMA((2 * KV + 1,)),
        ],
        compiler_params=pltpu.CompilerParams(vmem_limit_bytes=FULL << 20),
    )(key_matrix, value_matrix, segment)


def fetch_kernel(q_ref, c_ref, after_ref, q_out, c_out, sems):
    copies = [pltpu.make_async_copy(q_ref, q_out, sems.at[0]), pltpu.make_async_copy(c_ref, c_out, sems.at[1])]
    for copy in copies:
        copy.start()
    for copy in copies:
        copy.wait()


def fetch(queries, cotangent, after):
    return pl.pallas_call(
        fetch_kernel,
        in_specs=[HBM, HBM, HBM],
        out_specs=[VMEM, VMEM],
        out_shape=[jax.ShapeDtypeStruct(queries.shape, queries.dtype)] * 2,
        scratch_shapes=[pltpu.SemaphoreType.DMA((2,))],
        compiler_params=pltpu.CompilerParams(vmem_limit_bytes=16 << 20),
    )(queries, cotangent, after)


def loop(count, body, start, pairs):
    if pairs <= BUNDLE:
        return body(0, start)
    return lax.fori_loop(0, count, body, start)


def attend_kernel(pairs, begin, per, span_of_heads, lanes, prevs, here_ref, *refs):
    own = refs[:pairs]
    peer = refs[pairs : 2 * pairs]
    q_ref, c_ref, sq_ref = refs[2 * pairs : 2 * pairs + 3]
    refs = refs[2 * pairs + 3 + prevs :]
    low, high = span_of_heads
    out_ref, gq_ref = refs[:2]
    parts = refs[2:7]
    kv, mask, s_scr, p_scr, e_scr, probs_scr, slopes_scr, out_scr, gq_scr = refs[7:-3]
    cnt, order, sems = refs[-3:]
    rows = q_ref.shape[1]
    heads = q_ref.shape[2] // KV // D
    each = heads * D
    static = pairs <= BUNDLE
    wide = heads * rows
    two = 2 * rows
    tall = BUNDLE * two
    keys = mask.shape[0]
    scale = 1.0 / math.sqrt(D)
    power = scale * math.log2(math.e)
    here = here_ref[0]

    def columns(g):
        return pl.ds((begin + low + g) * each, each)

    seg_q = sq_ref[...].astype(jnp.float32)
    q_pos = here * rows + lax.broadcasted_iota(jnp.int32, (rows, rows), 1)
    local = lax.broadcasted_iota(jnp.int32, (rows, rows), 0)
    sources = [src for k in range(pairs) for src in (own[k], peer[k])]
    base = 2 * per * rows
    seg_rows = [src[base : base + 16, :].astype(jnp.float32)[:1] for src in sources]
    seg_rows.append(jnp.zeros((rows - len(sources), rows), jnp.float32))
    seg_cols = jnp.transpose(jnp.concatenate(seg_rows, axis=0))

    def masks(k):
        adds = []
        for lane in range(2):
            block = (here ^ lane) - 2 * k
            seg_k = seg_cols[:, 2 * k + lane : 2 * k + lane + 1]
            ok = (block * rows + local <= q_pos) & ((seg_k == seg_q) | (seg_k == 0.0)) & (block >= 0)
            adds.append(jnp.where(ok, 0.0, NEG))
        return adds

    def store(at, k, adds):
        for lane, src in enumerate((own[k], peer[k])):
            to = pl.ds(pl.multiple_of(at + lane * rows, rows), rows)
            mask[to, :] = adds[lane]
            for h in range(low, high):
                for part in range(2):
                    kv[h - low, part, to, :] = src[(2 * h + part) * rows : (2 * h + part + 1) * rows, :]

    if static:
        for k in range(pairs):
            store(k * two, k, masks(k))
    else:
        cnt[0] = 0
        for k in range(pairs):
            adds = masks(k)

            @pl.when(jnp.max(jnp.maximum(adds[0], adds[1])) == 0.0)
            def _():
                store(cnt[0] * two, k, adds)
                order[cnt[0]] = k
                cnt[0] = cnt[0] + 1

        def blank(t, carry):
            at = pl.ds(pl.multiple_of(t * two, two), two)
            mask[at, :] = jnp.full((two, rows), NEG, jnp.float32)
            kv[:, :, at, :] = jnp.zeros((high - low, 2, two, D), jnp.bfloat16)
            order[t] = -1
            return carry

        lax.fori_loop(cnt[0], pl.cdiv(cnt[0], BUNDLE) * BUNDLE, blank, 0)
        for ref in parts:
            wipe = slice(low * two, high * two)
            ref[:, wipe, :] = jnp.zeros((ref.shape[0], (high - low) * two, D), ref.dtype)
    bundles = None if static else pl.cdiv(cnt[0], BUNDLE)
    copies = []

    def send(src, ref, g, which):
        copy = pltpu.make_async_copy(src.at[g], ref.at[0, :, columns(g)], sems.at[2 * g + which])
        copy.start()
        copies.append(copy)

    def stack(ref, g):
        first = (begin + low + g) * heads
        return jnp.concatenate([ref[0, :, (first + h) * D : (first + h + 1) * D] for h in range(heads)], axis=0)

    def tile(t, j):
        step = tall // STEPS
        return pl.ds(pl.multiple_of(t * tall + j * step, step), step)

    def span_of(t):
        return pl.ds(pl.multiple_of(t * tall, tall), tall)

    def one_head(g):
        q_all = stack(q_ref, g)
        c_all = stack(c_ref, g)
        at = (low + g) * two
        for w in range(wide // lanes):
            cols = slice(w * lanes, (w + 1) * lanes)
            q_w, c_w = q_all[cols], c_all[cols]

            def scores(t, top, q_w=q_w, c_w=c_w):
                span = span_of(t)
                s = dot(kv[g, 0, span, :], q_w, NT)
                s = s + jnp.concatenate([mask[span, :]] * (lanes // rows), axis=1)
                s_scr[span, :] = s
                p_scr[span, :] = dot(kv[g, 1, span, :], c_w, NT)
                top = jnp.maximum(top, jnp.max(s, axis=0, keepdims=True))
                return top

            top = loop(bundles, scores, jnp.full((1, lanes), NEG, jnp.float32), pairs)

            def forward(t, carry, top=top):
                total, delta, acc = carry
                for j in range(STEPS):
                    at = tile(t, j)
                    e = jnp.exp2((s_scr[at, :] - top) * power)
                    s_scr[at, :] = e
                    e_scr[at, :] = e.astype(jnp.bfloat16)
                    total = total + jnp.sum(e, axis=0, keepdims=True)
                    delta = delta + jnp.sum(e * p_scr[at, :], axis=0, keepdims=True)
                span = span_of(t)
                return total, delta, acc + dot(kv[g, 1, span, :], e_scr[span, :], TN)

            row = jnp.zeros((1, lanes), jnp.float32)
            total, delta, acc = loop(bundles, forward, (row, row, jnp.zeros((D, lanes), jnp.float32)), pairs)
            inverse = 1.0 / total
            delta = delta * inverse
            acc = acc * inverse
            for h in range(lanes // rows):
                to = slice((w * lanes // rows + h) * D, (w * lanes // rows + h + 1) * D)
                out_scr[g, :, to] = jnp.transpose(acc[:, h * rows : (h + 1) * rows]).astype(jnp.bfloat16)

            def backward(t, acc, inverse=inverse, delta=delta, cols=cols):
                for j in range(STEPS):
                    at = tile(t, j)
                    probs = s_scr[at, :] * inverse
                    probs_scr[at, cols] = probs.astype(jnp.bfloat16)
                    slopes_scr[at, cols] = (probs * (p_scr[at, :] - delta)).astype(jnp.bfloat16)
                span = span_of(t)
                return acc + dot(kv[g, 0, span, :], slopes_scr[span, cols], TN)

            grad = loop(bundles, backward, jnp.zeros((D, lanes), jnp.float32), pairs) * scale
            for h in range(lanes // rows):
                to = slice((w * lanes // rows + h) * D, (w * lanes // rows + h + 1) * D)
                gq_scr[g, :, to] = jnp.transpose(grad[:, h * rows : (h + 1) * rows])

        send(out_scr, out_ref, g, 0)
        send(gq_scr, gq_ref, g, 1)

        def key_side(t, carry):
            span = span_of(t)
            all_v = dot(probs_scr[span, :], c_all, NN)
            all_k = dot(slopes_scr[span, :], q_all, NN) * scale
            for j in range(BUNDLE):
                k = None if static else order[t * BUNDLE + j]
                grad_v = all_v[j * two : (j + 1) * two]
                grad_k = all_k[j * two : (j + 1) * two]

                def keep(first, slot):
                    for lane in range(2):
                        ref = parts[min(first + lane, 4)]
                        slot = lane if first == 4 else slot
                        part = slice(lane * rows, (lane + 1) * rows)
                        ref[slot, pl.ds(at, rows), :] = grad_k[part].astype(ref.dtype)
                        ref[slot, pl.ds(at + rows, rows), :] = grad_v[part].astype(ref.dtype)

                if static:
                    keep(*((0, 0) if j == 0 else (4, 0) if j == pairs - 1 else (2, j - 1)))
                    continue
                pl.when(k == 0)(lambda: keep(0, 0))
                pl.when((k > 0) & (k < pairs - 1))(lambda: keep(2, k - 1))
                pl.when(k == pairs - 1)(lambda: keep(4, 0))
            return carry

        loop(bundles, key_side, 0, pairs)

    def interleaved(count):
        state = [{} for _ in range(count)]
        steps = range(STEPS)

        def offset(g):
            return g % 2 * keys

        def rows_of(g, j):
            step = keys // STEPS
            return slice(offset(g) + j * step, offset(g) + (j + 1) * step)

        def score(g, j):
            st = state[g]
            if j == 0:
                st["q"], st["c"] = stack(q_ref, g), stack(c_ref, g)
                st["top"] = jnp.full((1, wide), NEG, jnp.float32)
            at, to = tile(0, j), rows_of(g, j)
            s = dot(kv[g, 0, at, :], st["q"], NT)
            s = s + jnp.concatenate([mask[at, :]] * heads, axis=1)
            s_scr[to, :] = s
            p_scr[to, :] = dot(kv[g, 1, at, :], st["c"], NT)
            st["top"] = jnp.maximum(st["top"], jnp.max(s, axis=0, keepdims=True))

        def weigh(g, j):
            st, to = state[g], rows_of(g, j)
            e = jnp.exp2((s_scr[to, :] - st["top"]) * power)
            s_scr[to, :] = e
            e_scr[to, :] = e.astype(jnp.bfloat16)
            total = jnp.sum(e, axis=0, keepdims=True)
            delta = jnp.sum(e * p_scr[to, :], axis=0, keepdims=True)
            st["total"] = total if j == 0 else st["total"] + total
            st["delta"] = delta if j == 0 else st["delta"] + delta

        def outputs(g):
            st = state[g]
            st["inverse"] = 1.0 / st["total"]
            st["delta"] = st["delta"] * st["inverse"]
            acc = dot(kv[g, 1], e_scr[offset(g) : offset(g) + keys, :], TN) * st["inverse"]
            for h in range(heads):
                out = jnp.transpose(acc[:, h * rows : (h + 1) * rows])
                out_scr[g, :, h * D : (h + 1) * D] = out.astype(jnp.bfloat16)
            send(out_scr, out_ref, g, 0)

        def slope(g, j):
            st, to = state[g], rows_of(g, j)
            probs = s_scr[to, :] * st["inverse"]
            probs_scr[to, :] = probs.astype(jnp.bfloat16)
            slopes_scr[to, :] = (probs * (p_scr[to, :] - st["delta"])).astype(jnp.bfloat16)

        def query_side(g):
            grad = dot(kv[g, 0], slopes_scr[offset(g) : offset(g) + keys, :], TN) * scale
            for h in range(heads):
                gq_scr[g, :, h * D : (h + 1) * D] = jnp.transpose(grad[:, h * rows : (h + 1) * rows])
            send(gq_scr, gq_ref, g, 1)

        def key_side(g):
            st = state[g]
            span = slice(offset(g), offset(g) + keys)
            all_v = dot(probs_scr[span, :], st["c"], NN)
            all_k = dot(slopes_scr[span, :], st["q"], NN) * scale
            first = (low + g) * two
            for k in range(pairs):
                for lane in range(2):
                    base = 0 if k == 0 else 4 if k == pairs - 1 else 2
                    ref = parts[min(base + lane, 4)]
                    slot = 0 if k == 0 else lane if k == pairs - 1 else k - 1
                    part = slice(k * two + lane * rows, k * two + (lane + 1) * rows)
                    ref[slot, first : first + rows, :] = all_k[part].astype(ref.dtype)
                    ref[slot, first + rows : first + two, :] = all_v[part].astype(ref.dtype)

        for j in steps:
            score(0, j)
        for g in range(count):
            more = g + 1 < count
            if g == 0 or ORDER == 0:
                for j in steps:
                    weigh(g, j)
                    if more:
                        score(g + 1, j)
            elif more:
                for j in steps:
                    score(g + 1, j)
            outputs(g)
            for j in steps:
                slope(g, j)
            if ORDER == 1 and more:
                for j in steps:
                    weigh(g + 1, j)
            query_side(g)
            if ORDER == 2 and more:
                for j in steps:
                    weigh(g + 1, j)
            key_side(g)
            if ORDER == 3 and more:
                for j in steps:
                    weigh(g + 1, j)

    if static:
        interleaved(high - low)
    else:
        for g in range(high - low):
            one_head(g)
    for copy in copies:
        copy.wait()


def attend(begin, per, heads, here, own, peer, queries, cotangent, segment, prev, made):
    pairs = len(own)
    count = heads[1] - heads[0]
    _, rows, width = queries.shape
    each = width // KV
    wide = each // D * rows
    lanes = wide if pairs <= BUNDLE else LANES
    keys = pl.cdiv(pairs, BUNDLE) * BUNDLE * 2 * rows
    many = min(count, 2) if pairs <= BUNDLE else 1
    parts = [
        jax.ShapeDtypeStruct((count, per * 2 * rows, D), dtype)
        for count, dtype in (
            (1, jnp.float32),
            (1, jnp.float32),
            (pairs - 2, jnp.float32),
            (pairs - 2, jnp.bfloat16),
            (2, jnp.bfloat16),
        )
    ]
    args = [here, *own, *peer, queries, cotangent, segment]
    in_specs = [pl.BlockSpec(memory_space=pltpu.SMEM)] + [VMEM] * (2 * pairs) + [VMEM] * 3
    aliases = {}
    if prev is not None:
        aliases.update({len(args): 0, len(args) + 1: 1})
        args += list(prev)
        in_specs += [HBM] * 2
    if made is not None:
        aliases.update({len(args) + i: 2 + i for i in range(len(made))})
        args += list(made)
        in_specs += [VMEM] * len(made)
    macs = count * wide * 2 * rows * D * 6 * pairs
    return pl.pallas_call(
        functools.partial(attend_kernel, pairs, begin, per, heads, lanes, len(args) - 2 * pairs - 4),
        in_specs=in_specs,
        out_specs=[HBM, HBM] + [VMEM] * len(parts),
        out_shape=[
            jax.ShapeDtypeStruct(queries.shape, jnp.bfloat16),
            jax.ShapeDtypeStruct(queries.shape, jnp.float32),
            *parts,
        ],
        scratch_shapes=[
            pltpu.VMEM((count, 2, keys, D), jnp.bfloat16),
            pltpu.VMEM((keys, rows), jnp.float32),
            pltpu.VMEM((many * keys, lanes), jnp.float32),
            pltpu.VMEM((many * keys, lanes), jnp.float32),
            pltpu.VMEM((many * keys, lanes), jnp.bfloat16),
            pltpu.VMEM((many * keys, wide), jnp.bfloat16),
            pltpu.VMEM((many * keys, wide), jnp.bfloat16),
            pltpu.VMEM((count, rows, each), jnp.bfloat16),
            pltpu.VMEM((count, rows, each), jnp.float32),
            pltpu.SMEM((1,), jnp.int32),
            pltpu.SMEM((pl.cdiv(pairs, BUNDLE) * BUNDLE,), jnp.int32),
            pltpu.SemaphoreType.DMA((2 * count,)),
        ],
        input_output_aliases=aliases,
        compiler_params=pltpu.CompilerParams(vmem_limit_bytes=48 << 20),
        cost_estimate=pl.CostEstimate(flops=4 * macs, bytes_accessed=8 << 20, transcendentals=0),
    )(*args)


def add_kernel(mine_ref, got_ref, theirs_ref, last_ref, first_ref, *sends):
    first_ref[...] = (theirs_ref[0] + last_ref[1].astype(jnp.float32)).astype(jnp.bfloat16)
    for k, send in enumerate(sends):
        send[...] = (mine_ref[k] + got_ref[k].astype(jnp.float32)).astype(jnp.bfloat16)


def add_lanes(mine, got, theirs, last):
    count, tall, _ = mine.shape
    return pl.pallas_call(
        add_kernel,
        in_specs=[VMEM] * 4,
        out_specs=[VMEM] * (count + 1),
        out_shape=[jax.ShapeDtypeStruct((tall, D), jnp.bfloat16)] * (count + 1),
        cost_estimate=pl.CostEstimate(flops=mine.size, bytes_accessed=8 * mine.size, transcendentals=0),
        compiler_params=pltpu.CompilerParams(vmem_limit_bytes=48 << 20),
    )(mine, got, theirs, last)


def finish_kernel(pairs, *refs):
    ins, (gk_ref, gv_ref) = refs[:-2], refs[-2:]
    rows = gk_ref.shape[1]
    each = pairs + 1
    head = 0
    for c in range(len(ins) // each):
        mine, last, *others = ins[c * each : (c + 1) * each]
        for g in range(mine.shape[1] // (2 * rows)):
            cols = slice(head * D, (head + 1) * D)
            head += 1
            for part, out in enumerate((gk_ref, gv_ref)):
                span = slice((2 * g + part) * rows, (2 * g + part + 1) * rows)
                total = mine[0, span, :] + last[0, span, :].astype(jnp.float32)
                for ref in others:
                    total = total + ref[span, :].astype(jnp.float32)
                out[0, :, cols] = total


def per_device(size, queries, key_matrix, value_matrix, cotangent, segment):
    rows = queries.shape[1]
    pairs = size // 2
    here = lax.axis_index("ctx").astype(jnp.int32).reshape(1)

    def up(x, k):
        return lax.ppermute(x, "ctx", [(i, (i + 2 * k) % size) for i in range(size if ROUND else size - 2 * k)])

    def down(x, k):
        return lax.ppermute(x, "ctx", [((i + 2 * k) % size, i) for i in range(size if ROUND else size - 2 * k)])

    def swap(x):
        return lax.ppermute(x, "ctx", [(i, i ^ 1) for i in range(size)])

    def far(block, direct, meanwhile=()):
        own = [up(block, 1)]
        for k in range(2, pairs - 1):
            if direct:
                own.append(up(block, k))
                continue
            if k == 2 and meanwhile:
                own[0], *meanwhile = lax.optimization_barrier((own[0], *meanwhile))
            own.append(up(own[-1], 1))
        return [swap(block), *own, up(block, pairs - 1)], meanwhile

    def near(block, first):
        other, *mids, top = first
        return [block, *mids, top], [other, *(swap(x) for x in mids), up(other, pairs - 1)]

    finals = []
    blocks = list(pack(key_matrix, value_matrix, segment))
    begin = 0
    prev = None
    queries, cotangent = fetch(queries, cotangent, blocks[0])
    first, (queries, cotangent) = far(blocks[0], False, (queries, cotangent))

    def later(values, event):
        return lax.optimization_barrier((*values, event))[:-1]

    waiting = None

    def finish(waiting):
        mine_0, theirs_0, mine_mid, got, last = waiting
        lower, *mids = add_lanes(mine_mid, got, theirs_0, last)
        downs = [down(x, k) for k, x in enumerate(mids, 1)]
        finals.extend([mine_0, last, swap(lower), *downs])

    for c, per in enumerate(SPLIT):
        more = c + 1 < len(SPLIT)
        own, peer = near(blocks[c], first)
        if more:
            (block,) = later(blocks[c + 1 : c + 2], (own + peer)[TIE1])
            blocks[c + 1] = block
            first, _ = far(block, DIRECT)
        if waiting is not None:
            lower = finish(waiting)
            waiting = None
            if TIE3:
                prev = later(prev, lower)
        attended, grad_query, *made = attend(
            begin, per, (0, per), here, own, peer, queries, cotangent, segment, prev, None
        )
        prev = (attended, grad_query)
        if more and TIE2:
            first = list(later(first, made[0]))
        begin += per
        mine_0, theirs_0, mine_mid, theirs_mid, last = made
        waiting = [mine_0, theirs_0, mine_mid, swap(theirs_mid), down(last, pairs - 1)]
    finish(waiting)
    grads = pl.pallas_call(
        functools.partial(finish_kernel, pairs),
        in_specs=[VMEM] * len(finals),
        out_specs=[VMEM] * 2,
        compiler_params=pltpu.CompilerParams(vmem_limit_bytes=16 << 20),
        out_shape=[jax.ShapeDtypeStruct(key_matrix.shape, jnp.float32)] * 2,
    )(*finals)
    return (attended, grad_query, grads[0], grads[1])


def solution(mesh):
    wide = P(("groups", "dp"), "ctx", None)
    return jax.shard_map(
        functools.partial(per_device, mesh.shape["ctx"]),
        mesh=mesh,
        in_specs=(wide, wide, wide, wide, P(("groups", "dp"), "ctx")),
        out_specs=(wide, wide, wide, wide),
        check_vma=False,
    )
```
